256 devices in a mesh: star: 2 (over x_hi), blk: 128 (over x_lo, y, z, core).
Axes of the slice: x: 4 (x_hi: 2, x_lo: 2; x = x_hi * 2 + x_lo), y: 4, z: 8, core: 2. Of those that a mesh axis runs over, the one named last changes fastest.
Arguments:
- lapse_field: float32 [2048, 16, 256], P(('star', 'blk')), may hold values from 0.3 to 1
- conformal: float32 [2048, 16, 256], P(('star', 'blk')), may hold values from 0.5 to 1.5
- mean_curv: float32 [2048, 16, 256], P(('star', 'blk')), may hold values from -3 to 3
- conformal_metric: float32 [6, 2048, 16, 256], P(None, ('star', 'blk')), may hold values from -0.3 to 1.6, as said below
- traceless_curv: float32 [6, 2048, 16, 256], P(None, ('star', 'blk')), may hold values from -2 to 2
- shift_vector: float32 [3, 2048, 16, 256], P(None, ('star', 'blk')), may hold values from -3 to 3
- density: float32 [2, 2048, 16, 256], P('star', 'blk'), may hold values from 0.2 to 2
- momentum: float32 [2, 3, 2048, 16, 256], P('star', None, 'blk'), may hold values from -3 to 3
- energy: float32 [2, 2048, 16, 256], P('star', 'blk'), may hold values from 0.2 to 2
- velocity: float32 [2, 3, 2048, 16, 256], P('star', None, 'blk'), may hold values from -0.5 to 0.5
- pressure: float32 [2, 2048, 16, 256], P('star', 'blk'), may hold values from 0.05 to 0.5
Outputs:
- bssn_rhs: float32 [15, 2048, 16, 256], P(None, ('star', 'blk'))
- hydro_rhs: float32 [2, 5, 2048, 16, 256], P('star', None, 'blk')
The draws below stay inside these ranges and needn't reach their ends.
Inputs may be any that keep to these rules, and one draw needn't show every extreme that they name: `conformal_metric`: in every cell the symmetric matrix with rows (xx, xy, xz), (xy, yy, yz), (xz, yz, zz) has diagonal entries from 0.8 to 1.6 and off-diagonal entries from -0.3 to 0.3, and each diagonal entry exceeds the sum of the magnitudes of the other entries of its row.
All inputs are finite; a program needn't handle non-finite values.
Results may differ from the reference program's by a relative error of at most 0.0003.
Values sent between devices are 32-bit elements; how exact they have to be, the bound alone decides.
A program may use at most 128 MiB of HBM per device.

```python
import math
from functools import reduce
import jax
import jax.numpy as jnp
from jax import lax

CX = 8
CY = 16
CZ = 256
STARS = 2
NX = 2048
FX = 2048
N_BLK = 128


def draw_conformal_metric(key, part):
    diag_key, off_key = jax.random.split(jax.random.fold_in(key, 11))
    cell_shape = (3, NX, CY, CZ)
    diagonal = jax.random.uniform(diag_key, cell_shape, jnp.float32, 0.8, 1.4)
    offdiag = jax.random.uniform(off_key, cell_shape, jnp.float32, -0.2, 0.2)
    return jnp.stack([diagonal[0], offdiag[0], offdiag[1], diagonal[1], offdiag[2], diagonal[2]], 0)


def steps_of(own_key, dims, pieces, smallest, high):
    def one(axis_at, blocks):
        steps = jax.random.uniform(jax.random.fold_in(jax.random.fold_in(own_key, 6), axis_at), (blocks,), jnp.float32, smallest / len(pieces), high / len(pieces))
        return jnp.repeat(jnp.exp(steps), dims[axis_at] // blocks).reshape((-1,) + (1,) * (len(dims) - axis_at - 1))

    level = one(*pieces[0])
    for cut in pieces[1:]:
        level = level * one(*cut)
    return level


def noise(rng, extent, spread, limit, shards=(), held_as=jnp.bfloat16):
    result = jax.random.normal(rng, extent, jnp.float32) * spread
    if len(shards) > 0:
        result = steps_of(rng, extent, shards, -0.22, 0.18) * result
    return jnp.clip(result, min=-limit, max=limit).astype(held_as)


def setup_inputs(seed: int = 0) -> dict:
    arg_keys = jax.random.split(jax.random.key(seed), 12)
    return {
        "lapse_field": jnp.clip(0.3 + 0.7 * jax.random.uniform(arg_keys[0], (NX, CY, CZ), jnp.float32) ** steps_of(arg_keys[0], (NX, CY, CZ), ((0, 256),), -0.2, 0.2), 0.3, 1.0),
        "conformal": jnp.clip(0.5 + 1.0 * jax.random.uniform(arg_keys[1], (NX, CY, CZ), jnp.float32) ** steps_of(arg_keys[1], (NX, CY, CZ), ((0, 256),), -0.2, 0.2), 0.5, 1.5),
        "mean_curv": noise(arg_keys[2], (NX, CY, CZ), 0.5, 3.0, ((0, 256),), jnp.float32),
        "conformal_metric": draw_conformal_metric(jax.random.fold_in(arg_keys[11], 71), 0),
        "traceless_curv": noise(arg_keys[4], (6, NX, CY, CZ), 0.3, 2.0, ((1, 256),), jnp.float32),
        "shift_vector": noise(arg_keys[5], (3, NX, CY, CZ), 0.5, 3.0, ((1, 256),), jnp.float32),
        "density": jnp.clip(jnp.exp(math.log(2.0) - 2.3025851 * jax.random.uniform(arg_keys[6], (STARS, FX, CY, CZ), jnp.float32) ** steps_of(arg_keys[6], (STARS, FX, CY, CZ), ((0, 2), (1, 128)), -0.2, 0.2)), 0.2, 2.0),
        "momentum": noise(arg_keys[7], (STARS, 3, FX, CY, CZ), 0.5, 3.0, ((0, 2), (2, 128)), jnp.float32),
        "energy": jnp.clip(jnp.exp(math.log(2.0) - 2.3025851 * jax.random.uniform(arg_keys[8], (STARS, FX, CY, CZ), jnp.float32) ** steps_of(arg_keys[8], (STARS, FX, CY, CZ), ((0, 2), (1, 128)), -0.2, 0.2)), 0.2, 2.0),
        "velocity": jnp.clip(jax.random.uniform(arg_keys[9], (STARS, 3, FX, CY, CZ), jnp.float32, -0.5, 0.5) * steps_of(arg_keys[9], (STARS, 3, FX, CY, CZ), ((0, 2), (2, 128)), -0.4, 0.0), -0.5, 0.5),
        "pressure": jnp.clip(jnp.exp(math.log(0.5) - 2.3025851 * jax.random.uniform(arg_keys[10], (STARS, FX, CY, CZ), jnp.float32) ** steps_of(arg_keys[10], (STARS, FX, CY, CZ), ((0, 2), (1, 128)), -0.2, 0.2)), 0.05, 0.5),
    }


pair_index = ((0, 1, 2), (1, 3, 4), (2, 4, 5))
sym_pairs = ((0, 0), (0, 1), (0, 2), (1, 1), (1, 2), (2, 2))
weno_eps = 1e-6


def accumulate(terms):
    return reduce(lambda x, y: x + y, terms)


def xfirst(values):
    return (values[..., 0:-4, :, :] - 8.0 * values[..., 1:-3, :, :] + 8.0 * values[..., 3:-1, :, :] - values[..., 4:, :, :]) / 12.0


def xsecond(values):
    return (-values[..., 0:-4, :, :] + 16.0 * values[..., 1:-3, :, :] - 30.0 * values[..., 2:-2, :, :] + 16.0 * values[..., 3:-1, :, :] - values[..., 4:, :, :]) / 12.0


def rfirst(values, direction):
    return (jnp.roll(values, 2, direction) - 8.0 * jnp.roll(values, 1, direction) + 8.0 * jnp.roll(values, -1, direction) - jnp.roll(values, -2, direction)) / 12.0


def rsecond(values, direction):
    return (-jnp.roll(values, 2, direction) + 16.0 * jnp.roll(values, 1, direction) - 30.0 * values + 16.0 * jnp.roll(values, -1, direction) - jnp.roll(values, -2, direction)) / 12.0


def bssn_rates(padded, sources):
    core_cells = padded[:, 2:-2]
    gradients = (xfirst(padded), rfirst(core_cells, -2), rfirst(core_cells, -1))
    lapse_core = core_cells[0]
    conf_core = core_cells[1]
    mean_core = core_cells[2]
    shift_core = core_cells[15:18]
    advected = shift_core[0] * gradients[0][:15] + shift_core[1] * gradients[1][:15] + shift_core[2] * gradients[2][:15]

    def metric_at(i, j):
        return core_cells[3 + pair_index[i][j]]

    def curv_at(i, j):
        return core_cells[9 + pair_index[i][j]]

    def dshift(k, i):
        return gradients[k][15 + i]

    div_shift = dshift(0, 0) + dshift(1, 1) + dshift(2, 2)
    a, b, c, d, e, f = [core_cells[3 + n] for n in range(6)]
    cofactor = (d * f - e * e, c * e - b * f, b * e - c * d, a * f - c * c, b * c - a * e, a * d - b * b)
    determ = a * cofactor[0] + b * cofactor[1] + c * cofactor[2]
    inverse = [entry / determ for entry in cofactor]

    def inverse_at(i, j):
        return inverse[pair_index[i][j]]

    lapse_pad = padded[0]
    hessian = (xsecond(lapse_pad), xfirst(rfirst(lapse_pad, -2)), xfirst(rfirst(lapse_pad, -1)),
               rsecond(lapse_core, -2), rfirst(rfirst(lapse_core, -1), -2), rsecond(lapse_core, -1))

    def hess_at(i, j):
        return hessian[pair_index[i][j]]

    trace_hess = accumulate([inverse_at(i, j) * hess_at(i, j) for i in range(3) for j in range(3)])
    mixed_curv = [[accumulate([curv_at(i, l) * inverse_at(l, j) for l in range(3)]) for j in range(3)] for i in range(3)]
    square_trace = accumulate([mixed_curv[i][j] * mixed_curv[j][i] for i in range(3) for j in range(3)])
    lapse_rate = advected[0] - 2.0 * lapse_core * mean_core
    conf_rate = advected[1] + (2.0 / 3.0) * conf_core * (lapse_core * mean_core - div_shift)
    mean_rate = advected[2] - conf_core * trace_hess + lapse_core * (square_trace + mean_core * mean_core / 3.0) + 4.0 * math.pi * lapse_core * sources[0]
    metric_rates = []
    curv_rates = []
    for p, (i, j) in enumerate(sym_pairs):
        moved_metric = accumulate([metric_at(i, k) * dshift(j, k) + metric_at(j, k) * dshift(i, k) for k in range(3)])
        metric_rates.append(advected[3 + p] - 2.0 * lapse_core * curv_at(i, j) + moved_metric - (2.0 / 3.0) * metric_at(i, j) * div_shift)
        moved_curv = accumulate([curv_at(i, k) * dshift(j, k) + curv_at(j, k) * dshift(i, k) for k in range(3)])
        product = accumulate([mixed_curv[i][k] * curv_at(k, j) for k in range(3)])
        curv_rates.append(advected[9 + p] + lapse_core * (mean_core * curv_at(i, j) - 2.0 * product) + moved_curv
                          - (2.0 / 3.0) * curv_at(i, j) * div_shift - conf_core * (hess_at(i, j) - trace_hess * metric_at(i, j) / 3.0))
    return jnp.stack([lapse_rate, conf_rate, mean_rate] + metric_rates + curv_rates, 0)


def restrict(fine_cells):
    leading = fine_cells.shape[:-3]
    extent_x, extent_y, extent_z = fine_cells.shape[-3:]
    blocks = fine_cells.reshape(leading + (extent_x // 2, 2, extent_y // 2, 2, extent_z // 2, 2))
    return jnp.sum(blocks, axis=(-5, -3, -1)) * 0.125


def refine_axis(coarse, axis_index):
    cell_count = coarse.shape[axis_index] - 2
    center = lax.slice_in_dim(coarse, 1, cell_count + 1, axis=axis_index)
    lower_side = lax.slice_in_dim(coarse, 0, cell_count, axis=axis_index)
    upper_side = lax.slice_in_dim(coarse, 2, cell_count + 2, axis=axis_index)
    even_cells = 0.75 * center + 0.25 * lower_side
    odd_cells = 0.75 * center + 0.25 * upper_side
    stacked = jnp.stack([even_cells, odd_cells], axis_index + 1)
    new_shape = coarse.shape[:axis_index] + (2 * cell_count,) + coarse.shape[axis_index + 1:]
    return stacked.reshape(new_shape)


def prolong(window):
    return refine_axis(refine_axis(refine_axis(window, 1), 2), 3)


def split_fluxes(conserved, velocity, pressure, fine_metric):
    lapse_fine = fine_metric[0]
    shift_fine = fine_metric[1]
    conf_fine = fine_metric[2]
    transport = lapse_fine * velocity[0] - shift_fine
    weight = lapse_fine * conf_fine ** -1.5 * pressure
    flux_terms = jnp.stack([conserved[0] * transport, conserved[1] * transport + weight, conserved[2] * transport,
                            conserved[3] * transport, conserved[4] * transport + weight * velocity[0]], 0)
    max_speed = lapse_fine + jnp.abs(shift_fine)
    return jnp.concatenate([0.5 * (flux_terms + max_speed * conserved), 0.5 * (flux_terms - max_speed * conserved)], 0)


def weno_value(left_two, left_one, middle, right_one, right_two):
    guess_one = (2.0 * left_two - 7.0 * left_one + 11.0 * middle) / 6.0
    guess_two = (-left_one + 5.0 * middle + 2.0 * right_one) / 6.0
    guess_three = (2.0 * middle + 5.0 * right_one - right_two) / 6.0
    smooth_one = 13.0 / 12.0 * (left_two - 2.0 * left_one + middle) ** 2 + 0.25 * (left_two - 4.0 * left_one + 3.0 * middle) ** 2
    smooth_two = 13.0 / 12.0 * (left_one - 2.0 * middle + right_one) ** 2 + 0.25 * (left_one - right_one) ** 2
    smooth_three = 13.0 / 12.0 * (middle - 2.0 * right_one + right_two) ** 2 + 0.25 * (3.0 * middle - 4.0 * right_one + right_two) ** 2
    weight_one = 0.1 / (weno_eps + smooth_one) ** 2
    weight_two = 0.6 / (weno_eps + smooth_two) ** 2
    weight_three = 0.3 / (weno_eps + smooth_three) ** 2
    return (weight_one * guess_one + weight_two * guess_two + weight_three * guess_three) / (weight_one + weight_two + weight_three)


def weno_rates(ghosts):
    cell_count = ghosts.shape[1] - 6
    plus_part = ghosts[:5]
    minus_part = ghosts[5:]

    def taps(values, start):
        return values[:, start:start + cell_count + 1]

    face_flux = weno_value(taps(plus_part, 0), taps(plus_part, 1), taps(plus_part, 2), taps(plus_part, 3), taps(plus_part, 4)) \
        + weno_value(taps(minus_part, 5), taps(minus_part, 4), taps(minus_part, 3), taps(minus_part, 2), taps(minus_part, 1))
    return (face_flux[:, :-1] - face_flux[:, 1:]) * 2.0


def reference(lapse_field, conformal, mean_curv, conformal_metric, traceless_curv, shift_vector, density, momentum, energy, velocity, pressure):
    metric_state = jnp.concatenate([lapse_field[None], conformal[None], mean_curv[None], conformal_metric, traceless_curv, shift_vector], 0)
    source_fine = energy + density + (momentum[:, 0] * velocity[:, 0] + momentum[:, 1] * velocity[:, 1] + momentum[:, 2] * velocity[:, 2]) + 3.0 * pressure
    source_coarse = restrict(source_fine)
    joined = source_coarse.reshape(NX, CY // 2, CZ // 2)
    source_level = jnp.roll(joined, 1, axis=0)
    source_level = jnp.pad(source_level, ((0, 0), (CY // 4, CY // 4), (CZ // 4, CZ // 4)))[None]
    slab_count = NX // CX
    slab_ids = jnp.arange(slab_count, dtype=jnp.int32)

    def metric_slab(slab_index):
        row_index = (slab_index * CX + jnp.arange(-2, CX + 2, dtype=jnp.int32)) % NX
        padded = jnp.take(metric_state, row_index, axis=1)
        sources = lax.dynamic_slice_in_dim(source_level, slab_index * CX, CX, 1)
        return bssn_rates(padded, sources)

    slab_rates = lax.map(metric_slab, slab_ids)
    bssn_rhs = slab_rates.transpose(1, 0, 2, 3, 4).reshape(15, NX, CY, CZ)

    coarse_three = jnp.stack([lapse_field, shift_vector[0], conformal], 0)
    shifted = jnp.roll(coarse_three, -1, axis=1)
    extended = jnp.concatenate([shifted[:, -1:], shifted, shifted[:, :1]], 1)
    extended = extended[:, :, CY // 4 - 1:3 * CY // 4 + 1, CZ // 4 - 1:3 * CZ // 4 + 1]

    def fine_slab(slab_index):
        return prolong(lax.dynamic_slice_in_dim(extended, slab_index * CX, CX + 2, 1))

    fine_blocks = lax.map(fine_slab, slab_ids)
    fine_metric = fine_blocks.reshape(STARS, N_BLK, 3, 2 * CX, CY, CZ).transpose(0, 2, 1, 3, 4, 5).reshape(STARS, 3, FX, CY, CZ)
    conserved = jnp.concatenate([density[:, None], momentum, energy[:, None]], 1)
    split_flux = jax.vmap(split_fluxes)(conserved, velocity, pressure, fine_metric)

    def hydro_slab(slab_index):
        star_index = slab_index // N_BLK
        block_index = slab_index % N_BLK
        row_index = block_index * (2 * CX) + jnp.arange(-3, 2 * CX + 3, dtype=jnp.int32)
        inside = (row_index >= 0) & (row_index < FX)
        clipped = jnp.clip(row_index, 0, FX - 1)
        star_flux = lax.dynamic_index_in_dim(split_flux, star_index, 0, keepdims=False)
        gathered = jnp.take(star_flux, clipped, axis=1)
        ghosts = jnp.where(inside[:, None, None], gathered, jnp.zeros_like(gathered))
        return weno_rates(ghosts)

    hydro_blocks = lax.map(hydro_slab, slab_ids)
    hydro_rhs = hydro_blocks.reshape(STARS, N_BLK, 5, 2 * CX, CY, CZ).transpose(0, 2, 1, 3, 4, 5).reshape(STARS, 5, FX, CY, CZ)
    return bssn_rhs, hydro_rhs
```

```python
import functools
import math

import jax
import jax.numpy as jnp
from jax import lax
from jax.experimental import pallas as pl
from jax.experimental.pallas import tpu as pltpu
from jax.sharding import PartitionSpec as P

MESH = pl.DeviceIdType.MESH
F32 = jnp.float32
EXACT = lax.Precision.HIGHEST

pair_index = ((0, 1, 2), (1, 3, 4), (2, 4, 5))
sym_pairs = ((0, 0), (0, 1), (0, 2), (1, 1), (1, 2), (2, 2))

LAPSE, CONF, CURV, METRIC, TRACE, SHIFT = 0, 1, 2, 3, 9, 15
COARSE, FINE = 8, 16
CY, CZ = 16, 256
LANES = 128


def total(terms):
    return functools.reduce(lambda x, y: x + y, terms)


def ring_first(v, axis):
    n = v.shape[axis]
    far = pltpu.roll(v, 2, axis) - pltpu.roll(v, n - 2, axis)
    near = pltpu.roll(v, n - 1, axis) - pltpu.roll(v, 1, axis)
    return far + 8.0 * near


def ring_second(v, axis):
    n = v.shape[axis]
    far = pltpu.roll(v, 2, axis) + pltpu.roll(v, n - 2, axis)
    near = pltpu.roll(v, n - 1, axis) + pltpu.roll(v, 1, axis)
    return 16.0 * near - far - 30.0 * v


def x_first(mp, f, r):
    return (mp[f, r - 2] - mp[f, r + 2]) + 8.0 * (mp[f, r + 1] - mp[f, r - 1])


def derivatives(mp, ob, dd, i):
    r = i + 2
    by12 = mp[SHIFT + 1, r] * (1.0 / 12.0)
    bz12 = mp[SHIFT + 2, r] * (1.0 / 12.0)
    for f in range(2, SHIFT):
        v = mp[f, r]
        ob[f, i] = by12 * ring_first(v, 0) + bz12 * ring_first(v, 1)
    bx12 = mp[SHIFT, r] * (1.0 / 12.0)
    for f in (LAPSE, CONF):
        v = mp[f, r]
        along = x_first(mp, f, r)
        ob[f, i] = bx12 * along + by12 * ring_first(v, 0) + bz12 * ring_first(v, 1)
        if f == LAPSE:
            dd[10] = ring_first(along, 0) * (1.0 / 144.0)
            dd[11] = ring_first(along, 1) * (1.0 / 144.0)
    v = mp[LAPSE, r]
    dd[9] = (16.0 * (mp[LAPSE, r - 1] + mp[LAPSE, r + 1]) - (mp[LAPSE, r - 2] + mp[LAPSE, r + 2]) - 30.0 * v) * (1.0 / 12.0)
    dd[12] = ring_second(v, 0) * (1.0 / 12.0)
    dd[13] = ring_first(ring_first(v, 1), 0) * (1.0 / 144.0)
    dd[14] = ring_second(v, 1) * (1.0 / 12.0)
    for k in range(3):
        v = mp[SHIFT + k, r]
        dd[k] = x_first(mp, SHIFT + k, r) * (1.0 / 12.0)
        dd[3 + k] = ring_first(v, 0) * (1.0 / 12.0)
        dd[6 + k] = ring_first(v, 1) * (1.0 / 12.0)


def rates(mp, ob, dd, i, tile):
    r = i + 2
    al, ch, kk = [mp[(f, r) + tile] for f in (LAPSE, CONF, CURV)]
    g = [mp[(METRIC + p, r) + tile] for p in range(6)]
    ds = [[dd[(3 * k + j,) + tile] for j in range(3)] for k in range(3)]
    hess = [dd[(9 + p,) + tile] for p in range(6)]
    div = ds[0][0] + ds[1][1] + ds[2][2]
    tdiv = div * (2.0 / 3.0)
    a, b, c, d, e, f = g
    cof = (d * f - e * e, c * e - b * f, b * e - c * d, a * f - c * c, b * c - a * e, a * d - b * b)
    rdet = 1.0 / (a * cof[0] + b * cof[1] + c * cof[2])
    inv = [entry * rdet for entry in cof]
    alk = al * kk
    al2 = 2.0 * al
    ob[(0, i) + tile] = ob[(0, i) + tile] - 2.0 * alk
    ob[(1, i) + tile] = ob[(1, i) + tile] + (2.0 / 3.0) * ch * (alk - div)
    trh = (inv[0] * hess[0] + inv[3] * hess[3] + inv[5] * hess[5]) + 2.0 * (inv[1] * hess[1] + inv[2] * hess[2] + inv[4] * hess[4])
    cv = [mp[(TRACE + p, r) + tile] for p in range(6)]
    mixed = [[total([cv[pair_index[p][k]] * inv[pair_index[k][q]] for k in range(3)]) for q in range(3)] for p in range(3)]
    square = (mixed[0][0] * mixed[0][0] + mixed[1][1] * mixed[1][1] + mixed[2][2] * mixed[2][2]) + 2.0 * (
        mixed[0][1] * mixed[1][0] + mixed[0][2] * mixed[2][0] + mixed[1][2] * mixed[2][1]
    )
    chtr = ch * trh
    ob[(2, i) + tile] = ob[(2, i) + tile] - chtr + al * (square + kk * kk * (1.0 / 3.0))
    chtr3 = chtr * (1.0 / 3.0)
    scale = alk - tdiv
    for p, (x, y) in enumerate(sym_pairs):
        if x == y:
            moved_g = 2.0 * total([g[pair_index[x][k]] * ds[x][k] for k in range(3)])
            moved_c = 2.0 * total([cv[pair_index[x][k]] * ds[x][k] for k in range(3)])
        else:
            moved_g = total([g[pair_index[x][k]] * ds[y][k] + g[pair_index[y][k]] * ds[x][k] for k in range(3)])
            moved_c = total([cv[pair_index[x][k]] * ds[y][k] + cv[pair_index[y][k]] * ds[x][k] for k in range(3)])
        ob[(3 + p, i) + tile] = ob[(3 + p, i) + tile] - al2 * cv[p] + moved_g - tdiv * g[p]
        product = total([mixed[x][k] * cv[pair_index[k][y]] for k in range(3)])
        ob[(9 + p, i) + tile] = ob[(9 + p, i) + tile] + scale * cv[p] - al2 * product + moved_c - ch * hess[p] + chtr3 * g[p]


def advect_x(mp, ob, src, i):
    r = i + 2
    bx12 = mp[SHIFT, r] * (1.0 / 12.0)
    for f in range(2, SHIFT):
        moved = bx12 * x_first(mp, f, r)
        if f == CURV:
            moved = moved + (4.0 * math.pi) * mp[LAPSE, r] * src[i]
        ob[f, i] = ob[f, i] + moved


def split_flux(fl, fine, fpm, jj, keep):
    odd = jj % 2
    t = (jj + 1) // 2
    u = t + 1 - 2 * odd
    lapse, shift, conf = [0.75 * fine[m, t] + 0.25 * fine[m, u] for m in range(3)]
    vel, pres = fl[5, jj], fl[6, jj]
    root = lax.rsqrt(conf)
    weight = lapse * (root * root * root) * pres
    moved = lapse * vel - shift
    speed = lapse + jnp.abs(shift)
    plus = 0.5 * (moved + speed)
    minus = 0.5 * (moved - speed)
    half = 0.5 * weight
    extra = (None, half, None, None, half * vel)
    for n in range(5):
        v = fl[n, jj]
        fp, fm = v * plus, v * minus
        if extra[n] is not None:
            fp, fm = fp + extra[n], fm + extra[n]
        if keep is not None:
            fp, fm = jnp.where(keep, fp, 0.0), jnp.where(keep, fm, 0.0)
        fpm[n, jj] = fp
        fpm[5 + n, jj] = fm


def cell_terms(v):
    e = [v[k + 1] - v[k] for k in range(len(v) - 1)]
    h, s0, s1, s2 = [None], [None], [None], [None]
    for k in range(1, len(v) - 1):
        hk = 0.5 * (e[k] - e[k - 1])
        ck = (13.0 / 3.0) * (hk * hk) + 1e-6
        tp, tm, mid = hk + e[k], hk - e[k - 1], e[k] - hk
        h.append(hk)
        s0.append(ck + tp * tp)
        s1.append(ck + mid * mid)
        s2.append(ck + tm * tm)
    return h, s0, s1, s2


def correction(s0, s1, s2, h0, h1, h2):
    p12, p02, p01 = s1 * s2, s0 * s2, s0 * s1
    w0, w1, w2 = p12 * p12, 6.0 * (p02 * p02), 3.0 * (p01 * p01)
    top = w0 * (2.0 * h0 - 3.0 * h1) - w1 * h1 - w2 * h2
    return top / (3.0 * (w0 + w1 + w2))


def weno(fpm, oh, first, faces, n, tile):
    layers = faces + 5
    fp = [fpm[(n, first + k) + tile] for k in range(layers)]
    fm = [fpm[(5 + n, first + k) + tile] for k in range(layers)]
    hp, p0, p1, p2 = cell_terms(fp)
    hm, m0, m1, m2 = cell_terms(fm)
    flux = [fp[k] + fm[k] for k in range(2, layers - 2)]
    last = None
    for q in range(faces):
        k = q + 2
        face = 0.5 * (flux[q] + flux[q + 1])
        face = face + correction(p0[k - 1], p1[k], p2[k + 1], hp[k - 1], hp[k], hp[k + 1])
        face = face + correction(m2[k + 2], m1[k + 1], m0[k], hm[k + 2], hm[k + 1], hm[k])
        if last is not None:
            oh[(n, first + k - 3) + tile] = 2.0 * (last - face)
        last = face


def iota2(shape, dim):
    return lax.broadcasted_iota(jnp.int32, shape, dim)


def refine_weights(fine_pos, coarse_pos, start):
    center = start + fine_pos // 2
    side = center + 2 * (fine_pos % 2) - 1
    return jnp.where(coarse_pos == center, 0.75, jnp.where(coarse_pos == side, 0.25, 0.0)).astype(F32)


def make_fine(mp, fine, py, pz):
    for m, f in enumerate((LAPSE, SHIFT, CONF)):
        for part in range(2):
            coarse = mp[f, 1 + 6 * part : 7 + 6 * part].reshape(6 * CY, CZ)
            wide = jnp.dot(py[...], coarse, precision=EXACT, preferred_element_type=F32)
            wide = jnp.dot(wide, pz[...], precision=EXACT, preferred_element_type=F32)
            fine[m, 6 * part : 6 * part + 6] = wide.reshape(6, CY, CZ)


def make_sources(fl, vyz, summed, src, plane, ry, rz):
    def pair(c, _):
        cells = []
        for s in range(2):
            j = 2 * c + s
            q = j + 3
            dot = fl[1, q] * fl[5, q] + fl[2, q] * vyz[0, j] + fl[3, q] * vyz[1, j]
            cells.append(fl[4, q] + fl[0, q] + dot + 3.0 * fl[6, q])
        summed[c] = cells[0] + cells[1]
        return 0

    lax.fori_loop(0, COARSE, pair, 0)
    level = jnp.dot(summed[...].reshape(COARSE * CY, CZ), rz[...], precision=EXACT, preferred_element_type=F32)
    level = jnp.dot(ry[...], level, precision=EXACT, preferred_element_type=F32).reshape(COARSE, CY, CZ)
    src[1:COARSE] = level[: COARSE - 1]
    plane[...] = level[COARSE - 1]


def kernel(sizes, lapse, conf, curv, metric, trace, shift, dens, mom, ener, vel, pres, ob, oh,
           mp, fl, vyz, src, plane, summed, dd, fine, fpm, py, pz, ry, rz, lsem, ssem, rsem):
    stars, blocks = sizes
    count = stars * blocks
    blk = lax.axis_index("blk")
    me = lax.axis_index("star") * blocks + blk
    up = lax.rem(me + 1, count)
    down = lax.rem(me + count - 1, count)
    up = (up // blocks, lax.rem(up, blocks))
    down = (down // blocks, lax.rem(down, blocks))

    barrier = pltpu.get_barrier_semaphore()
    for device in (up, down):
        pl.semaphore_signal(barrier, inc=1, device_id=device, device_id_type=MESH)

    own = pl.ds(2, COARSE)
    fown = pl.ds(3, FINE)
    loads = [
        pltpu.make_async_copy(source, target, lsem.at[k])
        for k, (source, target) in enumerate((
            (dens.at[0], fl.at[0, fown]),
            (mom.at[0], fl.at[pl.ds(1, 3), fown]),
            (ener.at[0], fl.at[4, fown]),
            (vel.at[0, 0], fl.at[5, fown]),
            (pres.at[0], fl.at[6, fown]),
            (vel.at[0, pl.ds(1, 2)], vyz),
            (shift, mp.at[pl.ds(SHIFT, 3), own]),
            (lapse, mp.at[LAPSE, own]),
            (conf, mp.at[CONF, own]),
            (curv, mp.at[CURV, own]),
            (metric, mp.at[pl.ds(METRIC, 6), own]),
            (trace, mp.at[pl.ds(TRACE, 6), own]),
        ))
    ]
    for copy in loads:
        copy.start()
    pl.semaphore_wait(barrier, 2)

    sends = []

    def send(source, target, device):
        k = len(sends)
        copy = pltpu.make_async_remote_copy(
            src_ref=source, dst_ref=target, send_sem=ssem.at[k], recv_sem=rsem.at[k], device_id=device, device_id_type=MESH
        )
        copy.start()
        sends.append(copy)
        return copy

    top, bottom = pl.ds(COARSE - 2, 2), pl.ds(0, 2)
    low, high = pl.ds(0, 2), pl.ds(COARSE + 2, 2)
    high3 = pl.ds(COARSE + 2, 3)
    ftop, flow, fhigh = pl.ds(FINE - 3, 3), pl.ds(0, 3), pl.ds(FINE + 3, 3)
    first = [
        send(shift.at[:, top], mp.at[pl.ds(SHIFT, 3), low], up),
        send(shift.at[0, flow], mp.at[SHIFT, high3], down),
        send(shift.at[pl.ds(1, 2), bottom], mp.at[pl.ds(SHIFT + 1, 2), high], down),
        send(lapse.at[top], mp.at[LAPSE, low], up),
        send(lapse.at[flow], mp.at[LAPSE, high3], down),
        send(conf.at[top], mp.at[CONF, low], up),
        send(conf.at[flow], mp.at[CONF, high3], down),
    ]
    second = []
    for source, target in (
        (lambda s: dens.at[0, s], lambda s: fl.at[0, s]),
        (lambda s: mom.at[0, :, s], lambda s: fl.at[pl.ds(1, 3), s]),
        (lambda s: ener.at[0, s], lambda s: fl.at[4, s]),
        (lambda s: vel.at[0, 0, s], lambda s: fl.at[5, s]),
        (lambda s: pres.at[0, s], lambda s: fl.at[6, s]),
    ):
        second.append(send(source(ftop), target(flow), up))
        second.append(send(source(flow), target(fhigh), down))
    third = [
        send(curv.at[top], mp.at[CURV, low], up),
        send(curv.at[bottom], mp.at[CURV, high], down),
        send(metric.at[:, top], mp.at[pl.ds(METRIC, 6), low], up),
        send(metric.at[:, bottom], mp.at[pl.ds(METRIC, 6), high], down),
        send(trace.at[:, top], mp.at[pl.ds(TRACE, 6), low], up),
        send(trace.at[:, bottom], mp.at[pl.ds(TRACE, 6), high], down),
    ]

    def same_block(shape):
        return iota2(shape, 0) // CY == iota2(shape, 1) // CY

    shape = (6 * CY, 6 * CY)
    py[...] = jnp.where(same_block(shape), refine_weights(iota2(shape, 0) % CY, iota2(shape, 1) % CY, CY // 4), 0.0)
    shape = (CZ, CZ)
    pz[...] = refine_weights(iota2(shape, 1), iota2(shape, 0), CZ // 4)
    rz[...] = jnp.where(CZ // 4 + iota2(shape, 0) // 2 == iota2(shape, 1), 0.125, 0.0).astype(F32)
    shape = (COARSE * CY, COARSE * CY)
    ry[...] = jnp.where(
        same_block(shape) & (CY // 4 + iota2(shape, 1) % CY // 2 == iota2(shape, 0) % CY), 1.0, 0.0
    ).astype(F32)

    for copy in loads[:6]:
        copy.wait()
    make_sources(fl, vyz, summed, src, plane, ry, rz)
    third.append(send(plane, src.at[0], up))
    for copy in loads[6:]:
        copy.wait()

    tiles = [(pl.ds(8 * y, 8), pl.ds(LANES * z, LANES)) for y in range(CY // 8) for z in range(CZ // LANES)]

    def tile_at(t):
        return (pl.ds(pl.multiple_of(t // 2 * 8, 8), 8), pl.ds(pl.multiple_of(t % 2 * LANES, LANES), LANES))

    def metric_layer(i):
        derivatives(mp, ob, dd, i)

        def one(t, _):
            rates(mp, ob, dd, i, tile_at(t))
            return 0

        lax.fori_loop(0, len(tiles), one, 0)

    def inner(i, _):
        metric_layer(i)
        advect_x(mp, ob, src, i)
        return 0

    def edge(k):
        return k + k // 2 * (COARSE - 4)

    def outer(k, _):
        metric_layer(edge(k))
        return 0

    def last(k, _):
        advect_x(mp, ob, src, edge(k))
        return 0

    lax.fori_loop(2, COARSE - 2, inner, 0)
    for copy in first:
        copy.wait_recv()
    lax.fori_loop(0, 4, outer, 0)
    make_fine(mp, fine, py, pz)

    def flux_own(jj, _):
        split_flux(fl, fine, fpm, jj, None)
        return 0

    lax.fori_loop(3, FINE + 3, flux_own, 0)

    def weno_inner(q, _):
        weno(fpm, oh, 3, FINE - 5, q // 4, tile_at(q % 4))
        return 0

    lax.fori_loop(0, 20, weno_inner, 0)

    for copy in second:
        copy.wait_recv()
    for jj in range(3):
        split_flux(fl, fine, fpm, jj, blk != 0)
        split_flux(fl, fine, fpm, FINE + 3 + jj, blk != blocks - 1)

    def weno_outer(q, _):
        weno(fpm, oh, 0, 4, q // 4, tile_at(q % 4))
        weno(fpm, oh, FINE - 3, 4, q // 4, tile_at(q % 4))
        return 0

    lax.fori_loop(0, 20, weno_outer, 0)

    for copy in third:
        copy.wait_recv()
    lax.fori_loop(0, 4, last, 0)
    for copy in sends:
        copy.wait_send()


def write_out(pb, ph, ob, oh, sem):
    copies = [pltpu.make_async_copy(pb, ob, sem.at[0]), pltpu.make_async_copy(ph, oh.at[0], sem.at[1])]
    for copy in copies:
        copy.start()
    for copy in copies:
        copy.wait()


def on_device(sizes, *arrays):
    hbm = pl.BlockSpec(memory_space=pltpu.HBM)
    vmem = pl.BlockSpec(memory_space=pltpu.VMEM)
    metric_out, fluid_out = (15, COARSE, CY, CZ), (5, FINE, CY, CZ)
    part = pl.pallas_call(
        functools.partial(kernel, sizes),
        out_shape=(pltpu.VMEM(metric_out, F32), pltpu.VMEM(fluid_out, F32)),
        in_specs=[hbm] * 11,
        out_specs=(vmem, vmem),
        scratch_shapes=[
            pltpu.VMEM((18, COARSE + 5, CY, CZ), F32),
            pltpu.VMEM((7, FINE + 6, CY, CZ), F32),
            pltpu.VMEM((2, FINE, CY, CZ), F32),
            pltpu.VMEM((COARSE, CY, CZ), F32),
            pltpu.VMEM((CY, CZ), F32),
            pltpu.VMEM((COARSE, CY, CZ), F32),
            pltpu.VMEM((15, CY, CZ), F32),
            pltpu.VMEM((3, 12, CY, CZ), F32),
            pltpu.VMEM((10, FINE + 6, CY, CZ), F32),
            pltpu.VMEM((6 * CY, 6 * CY), F32),
            pltpu.VMEM((CZ, CZ), F32),
            pltpu.VMEM((COARSE * CY, COARSE * CY), F32),
            pltpu.VMEM((CZ, CZ), F32),
            pltpu.SemaphoreType.DMA((12,)),
            pltpu.SemaphoreType.DMA((24,)),
            pltpu.SemaphoreType.DMA((24,)),
        ],
        compiler_params=pltpu.CompilerParams(collective_id=0, has_side_effects=True, vmem_limit_bytes=58 << 20),
        cost_estimate=pl.CostEstimate(flops=60_000_000, bytes_accessed=8_000_000, transcendentals=0),
    )(*arrays)
    anywhere = pl.BlockSpec(memory_space=pl.ANY)
    return pl.pallas_call(
        write_out,
        out_shape=(jax.ShapeDtypeStruct(metric_out, F32), jax.ShapeDtypeStruct((1,) + fluid_out, F32)),
        in_specs=[vmem] * 2,
        out_specs=(anywhere, anywhere),
        scratch_shapes=[pltpu.SemaphoreType.DMA((2,))],
        compiler_params=pltpu.CompilerParams(vmem_limit_bytes=16 << 20),
        cost_estimate=pl.CostEstimate(flops=0, bytes_accessed=6_400_000, transcendentals=0),
    )(*part)


def solution(mesh):
    level = P(("star", "blk"), None, None)
    level4 = P(None, ("star", "blk"), None, None)
    box = P("star", "blk", None, None)
    box5 = P("star", None, "blk", None, None)
    sizes = (mesh.shape["star"], mesh.shape["blk"])
    return jax.shard_map(
        functools.partial(on_device, sizes),
        mesh=mesh,
        in_specs=(level, level, level, level4, level4, level4, box, box5, box, box5, box),
        out_specs=(level4, box5),
        check_vma=False,
    )
```

```python
import functools
import math

import jax
import jax.numpy as jnp
from jax import lax
from jax.experimental import pallas as pl
from jax.experimental.pallas import tpu as pltpu
from jax.sharding import PartitionSpec as P

MESH = pl.DeviceIdType.MESH
F32 = jnp.float32

pair_index = ((0, 1, 2), (1, 3, 4), (2, 4, 5))
sym_pairs = ((0, 0), (0, 1), (0, 2), (1, 1), (1, 2), (2, 2))

LAPSE, CONF, CURV, METRIC, TRACE, SHIFT = 0, 1, 2, 3, 9, 15
COARSE, FINE = 8, 16
CY, CZ = 16, 256
LANES = 128


def total(terms):
    return functools.reduce(lambda x, y: x + y, terms)


def rolled(v, axis):
    n = v.shape[axis]
    if axis == 1:
        return [pltpu.roll(v, s, 1) for s in (2, 1, n - 1, n - 2)]
    low, high = v[:8], v[8:]
    row = iota2(low.shape, 0)
    out = []
    for s in (2, 1, 7, 6):
        a, b = pltpu.roll(low, s, 0), pltpu.roll(high, s, 0)
        wrapped = row < s
        if s < 4:
            parts = [jnp.where(wrapped, b, a), jnp.where(wrapped, a, b)]
        else:
            parts = [jnp.where(wrapped, a, b), jnp.where(wrapped, b, a)]
        out.append(jnp.concatenate(parts, 0))
    return out


def first_of(moved):
    return (moved[0] - moved[3]) + 8.0 * (moved[2] - moved[1])


def second_of(v, moved):
    return 16.0 * (moved[1] + moved[2]) - (moved[0] + moved[3]) - 30.0 * v


def ring_first(v, axis):
    return first_of(rolled(v, axis))


def x_first(mp, f, r):
    return (mp[f, r - 2] - mp[f, r + 2]) + 8.0 * (mp[f, r + 1] - mp[f, r - 1])


def derivatives(mp, ob, dd, i):
    r = i + 2
    by12 = mp[SHIFT + 1, r] * (1.0 / 12.0)
    bz12 = mp[SHIFT + 2, r] * (1.0 / 12.0)
    for f in range(2, SHIFT):
        v = mp[f, r]
        ob[f, i] = by12 * ring_first(v, 0) + bz12 * ring_first(v, 1)
    bx12 = mp[SHIFT, r] * (1.0 / 12.0)
    for f in (LAPSE, CONF):
        v = mp[f, r]
        along = x_first(mp, f, r)
        ys, zs = rolled(v, 0), rolled(v, 1)
        dz = first_of(zs)
        ob[f, i] = bx12 * along + by12 * first_of(ys) + bz12 * dz
        if f == LAPSE:
            dd[10] = ring_first(along, 0) * (1.0 / 144.0)
            dd[11] = ring_first(along, 1) * (1.0 / 144.0)
            dd[12] = second_of(v, ys) * (1.0 / 12.0)
            dd[13] = ring_first(dz, 0) * (1.0 / 144.0)
            dd[14] = second_of(v, zs) * (1.0 / 12.0)
    v = mp[LAPSE, r]
    dd[9] = (16.0 * (mp[LAPSE, r - 1] + mp[LAPSE, r + 1]) - (mp[LAPSE, r - 2] + mp[LAPSE, r + 2]) - 30.0 * v) * (1.0 / 12.0)
    for k in range(3):
        v = mp[SHIFT + k, r]
        dd[k] = x_first(mp, SHIFT + k, r) * (1.0 / 12.0)
        dd[3 + k] = ring_first(v, 0) * (1.0 / 12.0)
        dd[6 + k] = ring_first(v, 1) * (1.0 / 12.0)


def rates(mp, ob, dd, i, tile):
    r = i + 2
    al, ch, kk = [mp[(f, r) + tile] for f in (LAPSE, CONF, CURV)]
    g = [mp[(METRIC + p, r) + tile] for p in range(6)]
    ds = [[dd[(3 * k + j,) + tile] for j in range(3)] for k in range(3)]
    hess = [dd[(9 + p,) + tile] for p in range(6)]
    div = ds[0][0] + ds[1][1] + ds[2][2]
    tdiv = div * (2.0 / 3.0)
    a, b, c, d, e, f = g
    cof = (d * f - e * e, c * e - b * f, b * e - c * d, a * f - c * c, b * c - a * e, a * d - b * b)
    rdet = 1.0 / (a * cof[0] + b * cof[1] + c * cof[2])
    inv = [entry * rdet for entry in cof]
    alk = al * kk
    al2 = 2.0 * al
    ob[(0, i) + tile] = ob[(0, i) + tile] - 2.0 * alk
    ob[(1, i) + tile] = ob[(1, i) + tile] + (2.0 / 3.0) * ch * (alk - div)
    trh = (inv[0] * hess[0] + inv[3] * hess[3] + inv[5] * hess[5]) + 2.0 * (inv[1] * hess[1] + inv[2] * hess[2] + inv[4] * hess[4])
    cv = [mp[(TRACE + p, r) + tile] for p in range(6)]
    mixed = [[total([cv[pair_index[p][k]] * inv[pair_index[k][q]] for k in range(3)]) for q in range(3)] for p in range(3)]
    square = (mixed[0][0] * mixed[0][0] + mixed[1][1] * mixed[1][1] + mixed[2][2] * mixed[2][2]) + 2.0 * (
        mixed[0][1] * mixed[1][0] + mixed[0][2] * mixed[2][0] + mixed[1][2] * mixed[2][1]
    )
    chtr = ch * trh
    ob[(2, i) + tile] = ob[(2, i) + tile] - chtr + al * (square + kk * kk * (1.0 / 3.0))
    chtr3 = chtr * (1.0 / 3.0)
    scale = alk - tdiv
    for p, (x, y) in enumerate(sym_pairs):
        if x == y:
            moved_g = 2.0 * total([g[pair_index[x][k]] * ds[x][k] for k in range(3)])
            moved_c = 2.0 * total([cv[pair_index[x][k]] * ds[x][k] for k in range(3)])
        else:
            moved_g = total([g[pair_index[x][k]] * ds[y][k] + g[pair_index[y][k]] * ds[x][k] for k in range(3)])
            moved_c = total([cv[pair_index[x][k]] * ds[y][k] + cv[pair_index[y][k]] * ds[x][k] for k in range(3)])
        ob[(3 + p, i) + tile] = ob[(3 + p, i) + tile] - al2 * cv[p] + moved_g - tdiv * g[p]
        product = total([mixed[x][k] * cv[pair_index[k][y]] for k in range(3)])
        ob[(9 + p, i) + tile] = ob[(9 + p, i) + tile] + scale * cv[p] - al2 * product + moved_c - ch * hess[p] + chtr3 * g[p]


def advect_x(mp, ob, src, i):
    r = i + 2
    bx12 = mp[SHIFT, r] * (1.0 / 12.0)
    for f in range(2, SHIFT):
        moved = bx12 * x_first(mp, f, r)
        if f == CURV:
            moved = moved + (4.0 * math.pi) * mp[LAPSE, r] * src[i]
        ob[f, i] = ob[f, i] + moved


def split_flux(fl, fine, fpm, jj, keep):
    odd = jj % 2
    t = (jj + 1) // 2
    u = t + 1 - 2 * odd
    lapse, shift, conf = [0.75 * fine[m, t] + 0.25 * fine[m, u] for m in range(3)]
    vel, pres = fl[5, jj], fl[6, jj]
    root = lax.rsqrt(conf)
    weight = lapse * (root * root * root) * pres
    moved = lapse * vel - shift
    speed = lapse + jnp.abs(shift)
    plus = 0.5 * (moved + speed)
    minus = 0.5 * (moved - speed)
    half = 0.5 * weight
    extra = (None, half, None, None, half * vel)
    for n in range(5):
        v = fl[n, jj]
        fp, fm = v * plus, v * minus
        if extra[n] is not None:
            fp, fm = fp + extra[n], fm + extra[n]
        if keep is not None:
            fp, fm = jnp.where(keep, fp, 0.0), jnp.where(keep, fm, 0.0)
        fpm[n, jj] = fp
        fpm[5 + n, jj] = fm


def cell_terms(v):
    e = [v[k + 1] - v[k] for k in range(len(v) - 1)]
    d, z0, z1, z2 = [None], [None], [None], [None]
    for k in range(1, len(v) - 1):
        dk = e[k] - e[k - 1]
        mid = e[k] + e[k - 1]
        square = dk * dk
        flat = mid * mid + 4e-6
        s1 = flat + (13.0 / 3.0) * square
        both = flat + (25.0 / 3.0) * square
        cross = (4.0 * dk) * mid
        s0, s2 = both + cross, both - cross
        d.append(dk)
        z0.append(s0 * s0)
        z1.append(s1 * s1)
        z2.append(s2 * s2)
    return d, z0, z1, z2


def correction(z0, z1, z2, d0, d1, d2):
    w0, w1, w2 = 1.0 / z0, 2.0 / z1, 1.0 / z2
    top = w0 * ((2.0 / 3.0) * d0 - d1) - (w1 * d1 + w2 * d2)
    return top * (1.0 / (w0 + 3.0 * (w1 + w2)))


def weno(fpm, oh, n, tile):
    layers = FINE + 6
    fp = [fpm[(n, k) + tile] for k in range(layers)]
    fm = [fpm[(5 + n, k) + tile] for k in range(layers)]
    dp, p0, p1, p2 = cell_terms(fp)
    dm, m0, m1, m2 = cell_terms(fm)
    last = None
    for k in range(2, layers - 3):
        face = (fp[k] + fm[k]) + (fp[k + 1] + fm[k + 1])
        face = face + correction(p0[k - 1], p1[k], p2[k + 1], dp[k - 1], dp[k], dp[k + 1])
        face = face + correction(m2[k + 2], m1[k + 1], m0[k], dm[k + 2], dm[k + 1], dm[k])
        if last is not None:
            oh[(n, k - 3) + tile] = last - face
        last = face


def iota2(shape, dim):
    return lax.broadcasted_iota(jnp.int32, shape, dim)


def refine_weights(fine_pos, coarse_pos, start):
    center = start + fine_pos // 2
    side = center + 2 * (fine_pos % 2) - 1
    return jnp.where(coarse_pos == center, 0.75, jnp.where(coarse_pos == side, 0.25, 0.0)).astype(F32)


def thirds(v):
    high = v.astype(jnp.bfloat16)
    rest = v - high.astype(F32)
    mid = rest.astype(jnp.bfloat16)
    low = (rest - mid.astype(F32)).astype(jnp.bfloat16)
    return [high, mid, low]


def times(v, weights):
    return jnp.dot(jnp.concatenate(thirds(v), 1), weights, preferred_element_type=F32)


def applied(weights, v):
    return jnp.dot(weights, jnp.concatenate(thirds(v), 0), preferred_element_type=F32)


def make_fine(mp, fine, py, pz):
    for m, f in enumerate((LAPSE, SHIFT, CONF)):
        wide = times(mp[f, 1:13].reshape(12 * CY, CZ), pz[...])
        for part in range(3):
            rows = 4 * CY
            fine[m, 4 * part : 4 * part + 4] = applied(py[...], wide[rows * part : rows * part + rows]).reshape(4, CY, CZ)


def make_sources(fl, vyz, summed, src, plane, ry, rz):
    def pair(c, _):
        cells = []
        for s in range(2):
            j = 2 * c + s
            q = j + 3
            dot = fl[1, q] * fl[5, q] + fl[2, q] * vyz[0, j] + fl[3, q] * vyz[1, j]
            cells.append(fl[4, q] + fl[0, q] + dot + 3.0 * fl[6, q])
        summed[c] = cells[0] + cells[1]
        return 0

    lax.fori_loop(0, COARSE, pair, 0)
    level = times(summed[...].reshape(COARSE * CY, CZ), rz[...])
    level = applied(ry[...], level).reshape(COARSE, CY, CZ)
    src[1:COARSE] = level[: COARSE - 1]
    plane[...] = level[COARSE - 1]


def kernel(sizes, lapse, conf, curv, metric, trace, shift, dens, mom, ener, vel, pres, ob, oh,
           mp, fl, vyz, src, plane, summed, dd, fine, fpm, py, pz, ry, rz, lsem, ssem, rsem):
    stars, blocks = sizes
    count = stars * blocks
    blk = lax.axis_index("blk")
    me = lax.axis_index("star") * blocks + blk
    up = lax.rem(me + 1, count)
    down = lax.rem(me + count - 1, count)
    up = (up // blocks, lax.rem(up, blocks))
    down = (down // blocks, lax.rem(down, blocks))

    barrier = pltpu.get_barrier_semaphore()
    for device in (up, down):
        pl.semaphore_signal(barrier, inc=1, device_id=device, device_id_type=MESH)

    own = pl.ds(2, COARSE)
    fown = pl.ds(3, FINE)
    loads = [
        pltpu.make_async_copy(source, target, lsem.at[k])
        for k, (source, target) in enumerate((
            (dens.at[0], fl.at[0, fown]),
            (mom.at[0], fl.at[pl.ds(1, 3), fown]),
            (ener.at[0], fl.at[4, fown]),
            (vel.at[0, 0], fl.at[5, fown]),
            (pres.at[0], fl.at[6, fown]),
            (vel.at[0, pl.ds(1, 2)], vyz),
            (shift, mp.at[pl.ds(SHIFT, 3), own]),
            (lapse, mp.at[LAPSE, own]),
            (conf, mp.at[CONF, own]),
            (curv, mp.at[CURV, own]),
            (metric, mp.at[pl.ds(METRIC, 6), own]),
            (trace, mp.at[pl.ds(TRACE, 6), own]),
        ))
    ]
    for copy in loads:
        copy.start()
    pl.semaphore_wait(barrier, 2)

    sends = []

    def send(source, target, device):
        k = len(sends)
        copy = pltpu.make_async_remote_copy(
            src_ref=source, dst_ref=target, send_sem=ssem.at[k], recv_sem=rsem.at[k], device_id=device, device_id_type=MESH
        )
        copy.start()
        sends.append(copy)
        return copy

    top, bottom = pl.ds(COARSE - 2, 2), pl.ds(0, 2)
    low, high = pl.ds(0, 2), pl.ds(COARSE + 2, 2)
    high3 = pl.ds(COARSE + 2, 3)
    ftop, flow, fhigh = pl.ds(FINE - 3, 3), pl.ds(0, 3), pl.ds(FINE + 3, 3)
    first = [
        send(shift.at[:, top], mp.at[pl.ds(SHIFT, 3), low], up),
        send(shift.at[0, flow], mp.at[SHIFT, high3], down),
        send(shift.at[pl.ds(1, 2), bottom], mp.at[pl.ds(SHIFT + 1, 2), high], down),
        send(lapse.at[top], mp.at[LAPSE, low], up),
        send(lapse.at[flow], mp.at[LAPSE, high3], down),
        send(conf.at[top], mp.at[CONF, low], up),
        send(conf.at[flow], mp.at[CONF, high3], down),
    ]
    second = []
    for source, target in (
        (lambda s: dens.at[0, s], lambda s: fl.at[0, s]),
        (lambda s: mom.at[0, :, s], lambda s: fl.at[pl.ds(1, 3), s]),
        (lambda s: ener.at[0, s], lambda s: fl.at[4, s]),
        (lambda s: vel.at[0, 0, s], lambda s: fl.at[5, s]),
        (lambda s: pres.at[0, s], lambda s: fl.at[6, s]),
    ):
        second.append(send(source(ftop), target(flow), up))
        second.append(send(source(flow), target(fhigh), down))
    third = [
        send(curv.at[top], mp.at[CURV, low], up),
        send(curv.at[bottom], mp.at[CURV, high], down),
        send(metric.at[:, top], mp.at[pl.ds(METRIC, 6), low], up),
        send(metric.at[:, bottom], mp.at[pl.ds(METRIC, 6), high], down),
        send(trace.at[:, top], mp.at[pl.ds(TRACE, 6), low], up),
        send(trace.at[:, bottom], mp.at[pl.ds(TRACE, 6), high], down),
    ]

    def fill(ref, weights, shape):
        part = weights(iota2(shape, 0), iota2(shape, 1)).astype(jnp.bfloat16)
        wide = ref.shape[1] != shape[1]
        for k in range(3):
            if wide:
                ref[:, shape[1] * k : shape[1] * k + shape[1]] = part
            else:
                ref[shape[0] * k : shape[0] * k + shape[0], :] = part

    def in_block(r, c, weights):
        return jnp.where(r // CY == c // CY, weights, 0.0)

    fill(rz, lambda r, c: jnp.where(CZ // 4 + r // 2 == c, 0.125, 0.0), (CZ, CZ))
    fill(ry, lambda r, c: in_block(r, c, jnp.where(CY // 4 + c % CY // 2 == r % CY, 1.0, 0.0)), (COARSE * CY, COARSE * CY))
    fill(pz, lambda r, c: refine_weights(c, r, CZ // 4), (CZ, CZ))
    fill(py, lambda r, c: in_block(r, c, refine_weights(r % CY, c % CY, CY // 4)), (4 * CY, 4 * CY))

    for copy in loads[:6]:
        copy.wait()
    make_sources(fl, vyz, summed, src, plane, ry, rz)
    third.append(send(plane, src.at[0], up))
    for copy in loads[6:]:
        copy.wait()

    tiles = [(pl.ds(8 * y, 8), pl.ds(LANES * z, LANES)) for y in range(CY // 8) for z in range(CZ // LANES)]

    def tile_at(t):
        return (pl.ds(pl.multiple_of(t // 2 * 8, 8), 8), pl.ds(pl.multiple_of(t % 2 * LANES, LANES), LANES))

    def metric_layer(i):
        derivatives(mp, ob, dd, i)

        def one(t, _):
            rates(mp, ob, dd, i, tile_at(t))
            return 0

        lax.fori_loop(0, len(tiles), one, 0)

    def inner(i, _):
        metric_layer(i)
        advect_x(mp, ob, src, i)
        return 0

    def edge(k):
        return k + k // 2 * (COARSE - 4)

    def outer(k, _):
        metric_layer(edge(k))
        return 0

    def last(k, _):
        advect_x(mp, ob, src, edge(k))
        return 0

    lax.fori_loop(2, COARSE - 2, inner, 0)
    for copy in first:
        copy.wait_recv()
    lax.fori_loop(0, 4, outer, 0)
    make_fine(mp, fine, py, pz)

    def flux_own(jj, _):
        split_flux(fl, fine, fpm, jj, None)
        return 0

    lax.fori_loop(3, FINE + 3, flux_own, 0)

    for copy in second:
        copy.wait_recv()
    for jj in range(3):
        split_flux(fl, fine, fpm, jj, blk != 0)
        split_flux(fl, fine, fpm, FINE + 3 + jj, blk != blocks - 1)

    def faces(q, _):
        weno(fpm, oh, q // 4, tile_at(q % 4))
        return 0

    lax.fori_loop(0, 20, faces, 0)

    for copy in third:
        copy.wait_recv()
    lax.fori_loop(0, 4, last, 0)
    for copy in sends:
        copy.wait_send()


def write_out(pb, ph, ob, oh, sem):
    copies = [pltpu.make_async_copy(pb, ob, sem.at[0]), pltpu.make_async_copy(ph, oh.at[0], sem.at[1])]
    for copy in copies:
        copy.start()
    for copy in copies:
        copy.wait()


def on_device(sizes, *arrays):
    hbm = pl.BlockSpec(memory_space=pltpu.HBM)
    vmem = pl.BlockSpec(memory_space=pltpu.VMEM)
    metric_out, fluid_out = (15, COARSE, CY, CZ), (5, FINE, CY, CZ)
    part = pl.pallas_call(
        functools.partial(kernel, sizes),
        out_shape=(pltpu.VMEM(metric_out, F32), pltpu.VMEM(fluid_out, F32)),
        in_specs=[hbm] * 11,
        out_specs=(vmem, vmem),
        scratch_shapes=[
            pltpu.VMEM((18, COARSE + 5, CY, CZ), F32),
            pltpu.VMEM((7, FINE + 6, CY, CZ), F32),
            pltpu.VMEM((2, FINE, CY, CZ), F32),
            pltpu.VMEM((COARSE, CY, CZ), F32),
            pltpu.VMEM((CY, CZ), F32),
            pltpu.VMEM((COARSE, CY, CZ), F32),
            pltpu.VMEM((15, CY, CZ), F32),
            pltpu.VMEM((3, 12, CY, CZ), F32),
            pltpu.VMEM((10, FINE + 6, CY, CZ), F32),
            pltpu.VMEM((4 * CY, 3 * 4 * CY), jnp.bfloat16),
            pltpu.VMEM((3 * CZ, CZ), jnp.bfloat16),
            pltpu.VMEM((COARSE * CY, 3 * COARSE * CY), jnp.bfloat16),
            pltpu.VMEM((3 * CZ, CZ), jnp.bfloat16),
            pltpu.SemaphoreType.DMA((12,)),
            pltpu.SemaphoreType.DMA((24,)),
            pltpu.SemaphoreType.DMA((24,)),
        ],
        compiler_params=pltpu.CompilerParams(collective_id=0, has_side_effects=True, vmem_limit_bytes=58 << 20),
        cost_estimate=pl.CostEstimate(flops=60_000_000, bytes_accessed=8_000_000, transcendentals=0),
    )(*arrays)
    anywhere = pl.BlockSpec(memory_space=pl.ANY)
    return pl.pallas_call(
        write_out,
        out_shape=(jax.ShapeDtypeStruct(metric_out, F32), jax.ShapeDtypeStruct((1,) + fluid_out, F32)),
        in_specs=[vmem] * 2,
        out_specs=(anywhere, anywhere),
        scratch_shapes=[pltpu.SemaphoreType.DMA((2,))],
        compiler_params=pltpu.CompilerParams(vmem_limit_bytes=16 << 20),
        cost_estimate=pl.CostEstimate(flops=0, bytes_accessed=6_400_000, transcendentals=0),
    )(*part)


def solution(mesh):
    level = P(("star", "blk"), None, None)
    level4 = P(None, ("star", "blk"), None, None)
    box = P("star", "blk", None, None)
    box5 = P("star", None, "blk", None, None)
    sizes = (mesh.shape["star"], mesh.shape["blk"])
    return jax.shard_map(
        functools.partial(on_device, sizes),
        mesh=mesh,
        in_specs=(level, level, level, level4, level4, level4, box, box5, box, box5, box),
        out_specs=(level4, box5),
        check_vma=False,
    )
```

```python
import functools
import math

import jax
import jax.numpy as jnp
from jax import lax
from jax.experimental import pallas as pl
from jax.experimental.pallas import tpu as pltpu
from jax.sharding import PartitionSpec as P

MESH = pl.DeviceIdType.MESH
F32 = jnp.float32

pair_index = ((0, 1, 2), (1, 3, 4), (2, 4, 5))
sym_pairs = ((0, 0), (0, 1), (0, 2), (1, 1), (1, 2), (2, 2))

LAPSE, CONF, CURV, METRIC, TRACE, SHIFT = 0, 1, 2, 3, 9, 15
COARSE, FINE = 8, 16
CY, CZ = 16, 256
LANES = 128


def total(terms):
    return functools.reduce(lambda x, y: x + y, terms)


def rolled(v, axis):
    n = v.shape[axis]
    if axis == 1:
        return [pltpu.roll(v, s, 1) for s in (2, 1, n - 1, n - 2)]
    low, high = v[:8], v[8:]
    row = iota2(low.shape, 0)
    out = []
    for s in (2, 1, 7, 6):
        a, b = pltpu.roll(low, s, 0), pltpu.roll(high, s, 0)
        wrapped = row < s
        if s < 4:
            parts = [jnp.where(wrapped, b, a), jnp.where(wrapped, a, b)]
        else:
            parts = [jnp.where(wrapped, a, b), jnp.where(wrapped, b, a)]
        out.append(jnp.concatenate(parts, 0))
    return out


def halves(v):
    high = v.astype(jnp.bfloat16)
    return [high, (v - high.astype(F32)).astype(jnp.bfloat16)]


def stencil(to, source, n):
    ahead = (source - to) & (n - 1)
    near = jnp.where(ahead == 1, 8.0, jnp.where(ahead == n - 1, -8.0, 0.0))
    return jnp.where(ahead == 2, -1.0, jnp.where(ahead == n - 2, 1.0, near))


def first_of(moved):
    return (moved[0] - moved[3]) + 8.0 * (moved[2] - moved[1])


def second_of(v, moved):
    return 16.0 * (moved[1] + moved[2]) - (moved[0] + moved[3]) - 30.0 * v


def ring_first(v, axis):
    return first_of(rolled(v, axis))


def x_first(mp, f, r):
    return (mp[f, r - 2] - mp[f, r + 2]) + 8.0 * (mp[f, r + 1] - mp[f, r - 1])


def derivatives(mp, ob, dd, src, ysten, zsten, start, inner):
    fields = range(1, SHIFT + 3)
    layers = [start, start + 1]
    parts = [[halves(mp[f, i + 2]) for f in fields] for i in layers]
    flat = jnp.concatenate([jnp.concatenate(p, 1) for layer in parts for p in layer], 0)
    flat = jnp.dot(flat, zsten[...], preferred_element_type=F32)
    for slot, i in enumerate(layers):
        r = i + 2
        bx12, by12, bz12 = [mp[SHIFT + k, r] * (1.0 / 12.0) for k in range(3)]
        base = len(fields) * slot - 1
        dz = {f: flat[CY * (base + f) : CY * (base + f + 1)] for f in fields}
        dy = {f: jnp.dot(ysten[...], jnp.concatenate(parts[slot][f - 1], 0), preferred_element_type=F32) for f in fields}

        v = mp[LAPSE, r]
        along = x_first(mp, LAPSE, r)
        ys, zs = rolled(v, 0), rolled(v, 1)
        lapse_z = first_of(zs)
        ob[LAPSE, i] = bx12 * along + by12 * first_of(ys) + bz12 * lapse_z
        outer = (mp[LAPSE, r - 2] + mp[LAPSE, r + 2]) + 30.0 * v
        dd[slot, 9] = (16.0 * (mp[LAPSE, r - 1] + mp[LAPSE, r + 1]) - outer) * (1.0 / 12.0)
        dd[slot, 10] = ring_first(along, 0) * (1.0 / 144.0)
        dd[slot, 11] = ring_first(along, 1) * (1.0 / 144.0)
        dd[slot, 12] = second_of(v, ys) * (1.0 / 12.0)
        dd[slot, 13] = ring_first(lapse_z, 0) * (1.0 / 144.0)
        dd[slot, 14] = second_of(v, zs) * (1.0 / 12.0)
        for f in range(1, SHIFT):
            moved = by12 * dy[f] + bz12 * dz[f]
            if inner or f == CONF:
                moved = moved + bx12 * x_first(mp, f, r)
            if inner and f == CURV:
                moved = moved + (4.0 * math.pi) * v * src[i]
            ob[f, i] = moved
        for k in range(3):
            dd[slot, k] = x_first(mp, SHIFT + k, r) * (1.0 / 12.0)
            dd[slot, 3 + k] = dy[SHIFT + k] * (1.0 / 12.0)
            dd[slot, 6 + k] = dz[SHIFT + k] * (1.0 / 12.0)


def rates(mp, ob, dd, slot, i, tile):
    r = i + 2
    al, ch, kk = [mp[(f, r) + tile] for f in (LAPSE, CONF, CURV)]
    g = [mp[(METRIC + p, r) + tile] for p in range(6)]
    ds = [[dd[(slot, 3 * k + j) + tile] for j in range(3)] for k in range(3)]
    hess = [dd[(slot, 9 + p) + tile] for p in range(6)]
    div = ds[0][0] + ds[1][1] + ds[2][2]
    tdiv = div * (2.0 / 3.0)
    a, b, c, d, e, f = g
    cof = (d * f - e * e, c * e - b * f, b * e - c * d, a * f - c * c, b * c - a * e, a * d - b * b)
    rdet = 1.0 / (a * cof[0] + b * cof[1] + c * cof[2])
    inv = [entry * rdet for entry in cof]
    alk = al * kk
    al2 = 2.0 * al
    ob[(0, i) + tile] = ob[(0, i) + tile] - 2.0 * alk
    ob[(1, i) + tile] = ob[(1, i) + tile] + (2.0 / 3.0) * ch * (alk - div)
    trh = (inv[0] * hess[0] + inv[3] * hess[3] + inv[5] * hess[5]) + 2.0 * (inv[1] * hess[1] + inv[2] * hess[2] + inv[4] * hess[4])
    cv = [mp[(TRACE + p, r) + tile] for p in range(6)]
    mixed = [[total([cv[pair_index[p][k]] * inv[pair_index[k][q]] for k in range(3)]) for q in range(3)] for p in range(3)]
    square = (mixed[0][0] * mixed[0][0] + mixed[1][1] * mixed[1][1] + mixed[2][2] * mixed[2][2]) + 2.0 * (
        mixed[0][1] * mixed[1][0] + mixed[0][2] * mixed[2][0] + mixed[1][2] * mixed[2][1]
    )
    chtr = ch * trh
    ob[(2, i) + tile] = ob[(2, i) + tile] - chtr + al * (square + kk * kk * (1.0 / 3.0))
    chtr3 = chtr * (1.0 / 3.0)
    scale = alk - tdiv
    for p, (x, y) in enumerate(sym_pairs):
        if x == y:
            moved_g = 2.0 * total([g[pair_index[x][k]] * ds[x][k] for k in range(3)])
            moved_c = 2.0 * total([cv[pair_index[x][k]] * ds[x][k] for k in range(3)])
        else:
            moved_g = total([g[pair_index[x][k]] * ds[y][k] + g[pair_index[y][k]] * ds[x][k] for k in range(3)])
            moved_c = total([cv[pair_index[x][k]] * ds[y][k] + cv[pair_index[y][k]] * ds[x][k] for k in range(3)])
        ob[(3 + p, i) + tile] = ob[(3 + p, i) + tile] - al2 * cv[p] + moved_g - tdiv * g[p]
        product = total([mixed[x][k] * cv[pair_index[k][y]] for k in range(3)])
        ob[(9 + p, i) + tile] = ob[(9 + p, i) + tile] + scale * cv[p] - al2 * product + moved_c - ch * hess[p] + chtr3 * g[p]


def split_flux(fl, fine, fpm, jj, keep):
    odd = jj & 1
    t = (jj + 1) >> 1
    u = t + 1 - 2 * odd
    lapse, shift, conf = [0.75 * fine[m, t] + 0.25 * fine[m, u] for m in range(3)]
    vel, pres = fl[5, jj], fl[6, jj]
    root = lax.rsqrt(conf)
    weight = lapse * (root * root * root) * pres
    moved = lapse * vel - shift
    speed = lapse + jnp.abs(shift)
    plus = 0.5 * (moved + speed)
    minus = 0.5 * (moved - speed)
    half = 0.5 * weight
    extra = (None, half, None, None, half * vel)
    for n in range(5):
        v = fl[n, jj]
        fp, fm = v * plus, v * minus
        if extra[n] is not None:
            fp, fm = fp + extra[n], fm + extra[n]
        if keep is not None:
            fp, fm = jnp.where(keep, fp, 0.0), jnp.where(keep, fm, 0.0)
        fpm[n, jj] = fp
        fpm[5 + n, jj] = fm


def cell_terms(v):
    e = [v[k + 1] - v[k] for k in range(len(v) - 1)]
    d, z0, z1, z2 = [None], [None], [None], [None]
    for k in range(1, len(v) - 1):
        dk = e[k] - e[k - 1]
        mid = e[k] + e[k - 1]
        square = dk * dk
        flat = mid * mid + 4e-6
        s1 = flat + (13.0 / 3.0) * square
        both = flat + (25.0 / 3.0) * square
        cross = (4.0 * dk) * mid
        s0, s2 = both + cross, both - cross
        d.append(dk)
        z0.append(s0 * s0)
        z1.append(s1 * s1)
        z2.append(s2 * s2)
    return d, z0, z1, z2


def correction(z0, z1, z2, d0, d1, d2):
    w0, w1, w2 = 1.0 / z0, 2.0 / z1, 1.0 / z2
    top = w0 * ((2.0 / 3.0) * d0 - d1) - (w1 * d1 + w2 * d2)
    return top * (1.0 / (w0 + 3.0 * (w1 + w2)))


def weno(fpm, oh, n, tile):
    layers = FINE + 6
    fp = [fpm[(n, k) + tile] for k in range(layers)]
    fm = [fpm[(5 + n, k) + tile] for k in range(layers)]
    dp, p0, p1, p2 = cell_terms(fp)
    dm, m0, m1, m2 = cell_terms(fm)
    last = None
    for k in range(2, layers - 3):
        face = (fp[k] + fm[k]) + (fp[k + 1] + fm[k + 1])
        face = face + correction(p0[k - 1], p1[k], p2[k + 1], dp[k - 1], dp[k], dp[k + 1])
        face = face + correction(m2[k + 2], m1[k + 1], m0[k], dm[k + 2], dm[k + 1], dm[k])
        if last is not None:
            oh[(n, k - 3) + tile] = last - face
        last = face


def iota2(shape, dim):
    return lax.broadcasted_iota(jnp.int32, shape, dim)


def refine_weights(fine_pos, coarse_pos, start):
    center = start + (fine_pos >> 1)
    side = center + 2 * (fine_pos & 1) - 1
    return jnp.where(coarse_pos == center, 0.75, jnp.where(coarse_pos == side, 0.25, 0.0)).astype(F32)


def thirds(v):
    high = v.astype(jnp.bfloat16)
    rest = v - high.astype(F32)
    mid = rest.astype(jnp.bfloat16)
    low = (rest - mid.astype(F32)).astype(jnp.bfloat16)
    return [high, mid, low]


def times(v, weights):
    return jnp.dot(jnp.concatenate(thirds(v), 1), weights, preferred_element_type=F32)


def applied(weights, v):
    return jnp.dot(weights, jnp.concatenate(thirds(v), 0), preferred_element_type=F32)


def make_fine(mp, fine, py, pz, layers):
    for m, f in enumerate((LAPSE, SHIFT, CONF)):
        coarse = jnp.concatenate([mp[f, 1 + t] for t in layers], 0)
        wide = times(coarse, pz[...])
        for part in range(0, len(layers), 4):
            block = applied(py[...], wide[CY * part : CY * (part + 4)])
            for k in range(4):
                fine[m, layers[part + k]] = block[CY * k : CY * (k + 1)]


def make_sources(fl, vyz, summed, src, plane, ry, rz):
    def pair(c, _):
        cells = []
        for s in range(2):
            j = 2 * c + s
            q = j + 3
            dot = fl[1, q] * fl[5, q] + fl[2, q] * vyz[0, j] + fl[3, q] * vyz[1, j]
            cells.append(fl[4, q] + fl[0, q] + dot + 3.0 * fl[6, q])
        summed[c] = cells[0] + cells[1]
        return 0

    lax.fori_loop(0, COARSE, pair, 0)
    level = times(summed[...].reshape(COARSE * CY, CZ), rz[...])
    level = applied(ry[...], level).reshape(COARSE, CY, CZ)
    src[1:COARSE] = level[: COARSE - 1]
    plane[...] = level[COARSE - 1]


def kernel(sizes, lapse, conf, curv, metric, trace, shift, dens, mom, ener, vel, pres, ob, oh, mp, src,
           fl, vyz, plane, summed, dd, fine, fpm, py, pz, ry, rz, ysten, zsten, lsem, ssem, rsem):
    stars, blocks = sizes
    count = stars * blocks
    blk = lax.axis_index("blk")
    me = lax.axis_index("star") * blocks + blk
    up = lax.rem(me + 1, count)
    down = lax.rem(me + count - 1, count)
    up = (up // blocks, lax.rem(up, blocks))
    down = (down // blocks, lax.rem(down, blocks))

    barrier = pltpu.get_barrier_semaphore()
    for device in (up, down):
        pl.semaphore_signal(barrier, inc=1, device_id=device, device_id_type=MESH)

    pl.semaphore_wait(barrier, 2)

    sends = []

    def send(source, target, device):
        k = len(sends)
        copy = pltpu.make_async_remote_copy(
            src_ref=source, dst_ref=target, send_sem=ssem.at[k], recv_sem=rsem.at[k], device_id=device, device_id_type=MESH
        )
        copy.start()
        sends.append(copy)
        return copy

    top, bottom = pl.ds(COARSE - 2, 2), pl.ds(0, 2)
    low, high = pl.ds(0, 2), pl.ds(COARSE + 2, 2)
    bottom3, high3 = pl.ds(0, 3), pl.ds(COARSE + 2, 3)
    ftop, flow, fhigh = pl.ds(FINE - 3, 3), pl.ds(0, 3), pl.ds(FINE + 3, 2)
    first = [
        send(shift.at[:, top], mp.at[pl.ds(SHIFT, 3), low], up),
        send(shift.at[0, bottom3], mp.at[SHIFT, high3], down),
        send(shift.at[pl.ds(1, 2), bottom], mp.at[pl.ds(SHIFT + 1, 2), high], down),
        send(lapse.at[top], mp.at[LAPSE, low], up),
        send(lapse.at[bottom3], mp.at[LAPSE, high3], down),
        send(conf.at[top], mp.at[CONF, low], up),
        send(conf.at[bottom3], mp.at[CONF, high3], down),
    ]
    second = []
    for source, target in (
        (lambda s: dens.at[0, s], lambda s: fl.at[0, s]),
        (lambda s: mom.at[0, :, s], lambda s: fl.at[pl.ds(1, 3), s]),
        (lambda s: ener.at[0, s], lambda s: fl.at[4, s]),
        (lambda s: vel.at[0, 0, s], lambda s: fl.at[5, s]),
        (lambda s: pres.at[0, s], lambda s: fl.at[6, s]),
    ):
        second.append(send(source(ftop), target(flow), up))
        second.append(send(source(bottom), target(fhigh), down))

    own = pl.ds(2, COARSE)
    fown = pl.ds(3, FINE)
    loads = [
        pltpu.make_async_copy(source, target, lsem.at[k])
        for k, (source, target) in enumerate((
            (dens.at[0], fl.at[0, fown]),
            (mom.at[0], fl.at[pl.ds(1, 3), fown]),
            (ener.at[0], fl.at[4, fown]),
            (vel.at[0, 0], fl.at[5, fown]),
            (pres.at[0], fl.at[6, fown]),
            (vel.at[0, pl.ds(1, 2)], vyz),
            (shift, mp.at[pl.ds(SHIFT, 3), own]),
            (lapse, mp.at[LAPSE, own]),
            (conf, mp.at[CONF, own]),
            (curv, mp.at[CURV, own]),
            (metric, mp.at[pl.ds(METRIC, 6), own]),
            (trace, mp.at[pl.ds(TRACE, 6), own]),
        ))
    ]
    for copy in loads:
        copy.start()

    def fill(ref, weights, shape, copies=3):
        part = weights(iota2(shape, 0), iota2(shape, 1)).astype(jnp.bfloat16)
        wide = ref.shape[1] != shape[1]
        for k in range(copies):
            if wide:
                ref[:, shape[1] * k : shape[1] * k + shape[1]] = part
            else:
                ref[shape[0] * k : shape[0] * k + shape[0], :] = part

    def in_block(r, c, weights):
        return jnp.where((r ^ c) < CY, weights, 0.0)

    fill(rz, lambda r, c: jnp.where(CZ // 4 + (r >> 1) == c, 0.125, 0.0), (CZ, CZ))
    fill(ry, lambda r, c: in_block(r, c, jnp.where(CY // 4 + ((c & CY - 1) >> 1) == (r & CY - 1), 1.0, 0.0)), (COARSE * CY, COARSE * CY))
    fill(zsten, lambda r, c: stencil(c, r, CZ), (CZ, CZ), 2)
    fill(ysten, lambda r, c: stencil(r, c, CY), (CY, CY), 2)
    fill(pz, lambda r, c: refine_weights(c, r, CZ // 4), (CZ, CZ))
    fill(py, lambda r, c: in_block(r, c, refine_weights(r & CY - 1, c & CY - 1, CY // 4)), (4 * CY, 4 * CY))

    for copy in loads[:6]:
        copy.wait()
    make_sources(fl, vyz, summed, src, plane, ry, rz)
    for copy in loads[6:9]:
        copy.wait()
    make_fine(mp, fine, py, pz, tuple(range(1, 1 + COARSE)))

    def flux_own(jj, _):
        split_flux(fl, fine, fpm, jj, None)
        return 0

    lax.fori_loop(3, FINE, flux_own, 0)
    second.append(send(fpm.at[pl.ds(5, 5), 5], fpm.at[pl.ds(5, 5), FINE + 5], down))
    third = [
        send(plane, src.at[0], up),
        send(curv.at[top], mp.at[CURV, low], up),
        send(curv.at[bottom], mp.at[CURV, high], down),
        send(metric.at[:, top], mp.at[pl.ds(METRIC, 6), low], up),
        send(metric.at[:, bottom], mp.at[pl.ds(METRIC, 6), high], down),
        send(trace.at[:, top], mp.at[pl.ds(TRACE, 6), low], up),
        send(trace.at[:, bottom], mp.at[pl.ds(TRACE, 6), high], down),
    ]
    for copy in loads[9:]:
        copy.wait()

    def tile_at(t):
        return (pl.ds(pl.multiple_of((t >> 1) * 8, 8), 8), pl.ds(pl.multiple_of((t & 1) * LANES, LANES), LANES))

    def metric_layers(start, inner):
        derivatives(mp, ob, dd, src, ysten, zsten, start, inner)

        def pair(q, _):
            slot, y = q >> 1, q & 1
            for z in range(CZ // LANES):
                tile = (pl.ds(pl.multiple_of(8 * y, 8), 8), pl.ds(LANES * z, LANES))
                rates(mp, ob, dd, slot, start + slot, tile)
            return 0

        lax.fori_loop(0, 4, pair, 0)

    def inner(k, _):
        metric_layers(2 + 2 * k, True)
        return 0

    def outer(k, _):
        metric_layers(k * (COARSE - 2), False)
        return 0

    lax.fori_loop(0, COARSE // 2 - 2, inner, 0)
    for copy in first:
        copy.wait_recv()
    lax.fori_loop(0, 2, outer, 0)
    make_fine(mp, fine, py, pz, (0, 1 + COARSE, 2 + COARSE, 3 + COARSE))
    for jj in range(FINE, FINE + 3):
        split_flux(fl, fine, fpm, jj, None)

    for copy in second:
        copy.wait_recv()
    for jj in range(3):
        split_flux(fl, fine, fpm, jj, blk != 0)
    for jj in range(FINE + 3, FINE + 5):
        split_flux(fl, fine, fpm, jj, blk != blocks - 1)
    for n in range(5, 10):
        fpm[n, FINE + 5] = jnp.where(blk != blocks - 1, fpm[n, FINE + 5], 0.0)

    def faces(q, _):
        weno(fpm, oh, q >> 2, tile_at(q & 3))
        return 0

    lax.fori_loop(0, 20, faces, 0)

    for copy in third:
        copy.wait_recv()
    for copy in sends:
        copy.wait_send()


def write_out(pb, ph, mp, src, ob, oh, edge, sem):
    copies = []

    def put(source, target):
        copy = pltpu.make_async_copy(source, target, sem.at[len(copies)])
        copy.start()
        copies.append(copy)

    rest = SHIFT - CURV
    middle = pl.ds(2, COARSE - 4)
    put(pb.at[pl.ds(CURV, rest), middle], ob.at[pl.ds(CURV, rest), middle])
    put(ph, oh.at[0])
    put(pb.at[pl.ds(0, CURV)], ob.at[pl.ds(0, CURV)])
    for k, i in enumerate((0, 1, COARSE - 2, COARSE - 1)):
        r = i + 2
        bx12 = mp[SHIFT, r] * (1.0 / 12.0)
        for f in range(CURV, SHIFT):
            moved = bx12 * x_first(mp, f, r)
            if f == CURV:
                moved = moved + (4.0 * math.pi) * mp[LAPSE, r] * src[i]
            edge[f - CURV, k] = pb[f, i] + moved
        if k % 2:
            put(edge.at[:, pl.ds(k - 1, 2)], ob.at[pl.ds(CURV, rest), pl.ds(i - 1, 2)])
    for copy in copies:
        copy.wait()


def on_device(sizes, *arrays):
    hbm = pl.BlockSpec(memory_space=pltpu.HBM)
    vmem = pl.BlockSpec(memory_space=pltpu.VMEM)
    metric_out, fluid_out = (15, COARSE, CY, CZ), (5, FINE, CY, CZ)
    part = pl.pallas_call(
        functools.partial(kernel, sizes),
        out_shape=(
            pltpu.VMEM(metric_out, F32),
            pltpu.VMEM(fluid_out, F32),
            pltpu.VMEM((18, COARSE + 5, CY, CZ), F32),
            pltpu.VMEM((COARSE, CY, CZ), F32),
        ),
        in_specs=[hbm] * 11,
        out_specs=(vmem,) * 4,
        scratch_shapes=[
            pltpu.VMEM((7, FINE + 6, CY, CZ), F32),
            pltpu.VMEM((2, FINE, CY, CZ), F32),
            pltpu.VMEM((CY, CZ), F32),
            pltpu.VMEM((COARSE, CY, CZ), F32),
            pltpu.VMEM((2, 15, CY, CZ), F32),
            pltpu.VMEM((3, 12, CY, CZ), F32),
            pltpu.VMEM((10, FINE + 6, CY, CZ), F32),
            pltpu.VMEM((4 * CY, 3 * 4 * CY), jnp.bfloat16),
            pltpu.VMEM((3 * CZ, CZ), jnp.bfloat16),
            pltpu.VMEM((COARSE * CY, 3 * COARSE * CY), jnp.bfloat16),
            pltpu.VMEM((3 * CZ, CZ), jnp.bfloat16),
            pltpu.VMEM((CY, 2 * CY), jnp.bfloat16),
            pltpu.VMEM((2 * CZ, CZ), jnp.bfloat16),
            pltpu.SemaphoreType.DMA((12,)),
            pltpu.SemaphoreType.DMA((25,)),
            pltpu.SemaphoreType.DMA((25,)),
        ],
        compiler_params=pltpu.CompilerParams(collective_id=0, has_side_effects=True, vmem_limit_bytes=54 << 20),
        cost_estimate=pl.CostEstimate(flops=60_000_000, bytes_accessed=8_000_000, transcendentals=0),
    )(*arrays)
    anywhere = pl.BlockSpec(memory_space=pl.ANY)
    return pl.pallas_call(
        write_out,
        out_shape=(jax.ShapeDtypeStruct(metric_out, F32), jax.ShapeDtypeStruct((1,) + fluid_out, F32)),
        in_specs=[vmem] * 4,
        out_specs=(anywhere, anywhere),
        scratch_shapes=[pltpu.VMEM((SHIFT - CURV, 4, CY, CZ), F32), pltpu.SemaphoreType.DMA((5,))],
        compiler_params=pltpu.CompilerParams(vmem_limit_bytes=16 << 20),
        cost_estimate=pl.CostEstimate(flops=0, bytes_accessed=6_400_000, transcendentals=0),
    )(*part)


def solution(mesh):
    level = P(("star", "blk"), None, None)
    level4 = P(None, ("star", "blk"), None, None)
    box = P("star", "blk", None, None)
    box5 = P("star", None, "blk", None, None)
    sizes = (mesh.shape["star"], mesh.shape["blk"])
    return jax.shard_map(
        functools.partial(on_device, sizes),
        mesh=mesh,
        in_specs=(level, level, level, level4, level4, level4, box, box5, box, box5, box),
        out_specs=(level4, box5),
        check_vma=False,
    )
```

```python
import functools
import math

import jax
import jax.numpy as jnp
from jax import lax
from jax.experimental import pallas as pl
from jax.experimental.pallas import tpu as pltpu
from jax.sharding import PartitionSpec as P

MESH = pl.DeviceIdType.MESH
F32 = jnp.float32

pair_index = ((0, 1, 2), (1, 3, 4), (2, 4, 5))
sym_pairs = ((0, 0), (0, 1), (0, 2), (1, 1), (1, 2), (2, 2))

LAPSE, CONF, CURV, METRIC, TRACE, SHIFT = 0, 1, 2, 3, 9, 15
COARSE, FINE = 8, 16
CY, CZ = 16, 256
LANES = 128


def total(terms):
    return functools.reduce(lambda x, y: x + y, terms)


def rolled(v, axis):
    n = v.shape[axis]
    if axis == 1:
        return [pltpu.roll(v, s, 1) for s in (2, 1, n - 1, n - 2)]
    low, high = v[:8], v[8:]
    row = iota2(low.shape, 0)
    out = []
    for s in (2, 1, 7, 6):
        a, b = pltpu.roll(low, s, 0), pltpu.roll(high, s, 0)
        wrapped = row < s
        if s < 4:
            parts = [jnp.where(wrapped, b, a), jnp.where(wrapped, a, b)]
        else:
            parts = [jnp.where(wrapped, a, b), jnp.where(wrapped, b, a)]
        out.append(jnp.concatenate(parts, 0))
    return out


def halves(v):
    high = v.astype(jnp.bfloat16)
    return [high, (v - high.astype(F32)).astype(jnp.bfloat16)]


def stencil(to, source, n):
    ahead = (source - to) & (n - 1)
    near = jnp.where(ahead == 1, 8.0, jnp.where(ahead == n - 1, -8.0, 0.0))
    return jnp.where(ahead == 2, -1.0, jnp.where(ahead == n - 2, 1.0, near))


def first_of(moved):
    return (moved[0] - moved[3]) + 8.0 * (moved[2] - moved[1])


def second_of(v, moved):
    return 16.0 * (moved[1] + moved[2]) - (moved[0] + moved[3]) - 30.0 * v


def ring_first(v, axis):
    return first_of(rolled(v, axis))


def x_first(mp, f, r):
    return (mp[f, r - 2] - mp[f, r + 2]) + 8.0 * (mp[f, r + 1] - mp[f, r - 1])


def derivatives(mp, ob, dd, src, ysten, zsten, start, inner):
    fields = range(1, SHIFT + 3)
    layers = [start, start + 1]
    parts = [[halves(mp[f, i + 2]) for f in fields] for i in layers]
    flat = jnp.concatenate([jnp.concatenate(p, 1) for layer in parts for p in layer], 0)
    flat = jnp.dot(flat, zsten[...], preferred_element_type=F32)
    for slot, i in enumerate(layers):
        r = i + 2
        bx12, by12, bz12 = [mp[SHIFT + k, r] * (1.0 / 12.0) for k in range(3)]
        base = len(fields) * slot - 1
        dz = {f: flat[CY * (base + f) : CY * (base + f + 1)] for f in fields}
        dy = {f: jnp.dot(ysten[...], jnp.concatenate(parts[slot][f - 1], 0), preferred_element_type=F32) for f in fields}

        v = mp[LAPSE, r]
        along = x_first(mp, LAPSE, r)
        ys, zs = rolled(v, 0), rolled(v, 1)
        lapse_z = first_of(zs)
        ob[LAPSE, i] = bx12 * along + by12 * first_of(ys) + bz12 * lapse_z
        outer = (mp[LAPSE, r - 2] + mp[LAPSE, r + 2]) + 30.0 * v
        dd[slot, 9] = (16.0 * (mp[LAPSE, r - 1] + mp[LAPSE, r + 1]) - outer) * (1.0 / 12.0)
        dd[slot, 10] = ring_first(along, 0) * (1.0 / 144.0)
        dd[slot, 11] = ring_first(along, 1) * (1.0 / 144.0)
        dd[slot, 12] = second_of(v, ys) * (1.0 / 12.0)
        dd[slot, 13] = ring_first(lapse_z, 0) * (1.0 / 144.0)
        dd[slot, 14] = second_of(v, zs) * (1.0 / 12.0)
        for f in range(1, SHIFT):
            moved = by12 * dy[f] + bz12 * dz[f]
            if inner or f == CONF:
                moved = moved + bx12 * x_first(mp, f, r)
            if inner and f == CURV:
                moved = moved + (4.0 * math.pi) * v * src[i]
            ob[f, i] = moved
        for k in range(3):
            dd[slot, k] = x_first(mp, SHIFT + k, r) * (1.0 / 12.0)
            dd[slot, 3 + k] = dy[SHIFT + k] * (1.0 / 12.0)
            dd[slot, 6 + k] = dz[SHIFT + k] * (1.0 / 12.0)


def rates(mp, ob, dd, slot, i, tile):
    r = i + 2
    al, ch, kk = [mp[(f, r) + tile] for f in (LAPSE, CONF, CURV)]
    g = [mp[(METRIC + p, r) + tile] for p in range(6)]
    ds = [[dd[(slot, 3 * k + j) + tile] for j in range(3)] for k in range(3)]
    hess = [dd[(slot, 9 + p) + tile] for p in range(6)]
    div = ds[0][0] + ds[1][1] + ds[2][2]
    tdiv = div * (2.0 / 3.0)
    a, b, c, d, e, f = g
    cof = (d * f - e * e, c * e - b * f, b * e - c * d, a * f - c * c, b * c - a * e, a * d - b * b)
    rdet = 1.0 / (a * cof[0] + b * cof[1] + c * cof[2])
    inv = [entry * rdet for entry in cof]
    alk = al * kk
    al2 = 2.0 * al
    ob[(0, i) + tile] = ob[(0, i) + tile] - 2.0 * alk
    ob[(1, i) + tile] = ob[(1, i) + tile] + (2.0 / 3.0) * ch * (alk - div)
    trh = (inv[0] * hess[0] + inv[3] * hess[3] + inv[5] * hess[5]) + 2.0 * (inv[1] * hess[1] + inv[2] * hess[2] + inv[4] * hess[4])
    cv = [mp[(TRACE + p, r) + tile] for p in range(6)]
    mixed = [[total([cv[pair_index[p][k]] * inv[pair_index[k][q]] for k in range(3)]) for q in range(3)] for p in range(3)]
    square = (mixed[0][0] * mixed[0][0] + mixed[1][1] * mixed[1][1] + mixed[2][2] * mixed[2][2]) + 2.0 * (
        mixed[0][1] * mixed[1][0] + mixed[0][2] * mixed[2][0] + mixed[1][2] * mixed[2][1]
    )
    chtr = ch * trh
    ob[(2, i) + tile] = ob[(2, i) + tile] - chtr + al * (square + kk * kk * (1.0 / 3.0))
    chtr3 = chtr * (1.0 / 3.0)
    scale = alk - tdiv
    for p, (x, y) in enumerate(sym_pairs):
        if x == y:
            moved_g = 2.0 * total([g[pair_index[x][k]] * ds[x][k] for k in range(3)])
            moved_c = 2.0 * total([cv[pair_index[x][k]] * ds[x][k] for k in range(3)])
        else:
            moved_g = total([g[pair_index[x][k]] * ds[y][k] + g[pair_index[y][k]] * ds[x][k] for k in range(3)])
            moved_c = total([cv[pair_index[x][k]] * ds[y][k] + cv[pair_index[y][k]] * ds[x][k] for k in range(3)])
        ob[(3 + p, i) + tile] = ob[(3 + p, i) + tile] - al2 * cv[p] + moved_g - tdiv * g[p]
        product = total([mixed[x][k] * cv[pair_index[k][y]] for k in range(3)])
        ob[(9 + p, i) + tile] = ob[(9 + p, i) + tile] + scale * cv[p] - al2 * product + moved_c - ch * hess[p] + chtr3 * g[p]


def split_flux(fl, fine, fpm, jj):
    odd = jj & 1
    t = (jj + 1) >> 1
    u = t + 1 - 2 * odd
    lapse, shift, conf = [0.75 * fine[m, t] + 0.25 * fine[m, u] for m in range(3)]
    vel, pres = fl[5, jj], fl[6, jj]
    root = lax.rsqrt(conf)
    weight = lapse * (root * root * root) * pres
    moved = lapse * vel - shift
    speed = lapse + jnp.abs(shift)
    plus = 0.5 * (moved + speed)
    minus = 0.5 * (moved - speed)
    half = 0.5 * weight
    extra = (None, half, None, None, half * vel)
    for n in range(5):
        v = fl[n, jj]
        fp, fm = v * plus, v * minus
        if extra[n] is not None:
            fp, fm = fp + extra[n], fm + extra[n]
        fpm[n, jj] = fp
        fpm[5 + n, jj] = fm


def cell_terms(v):
    e = [v[k + 1] - v[k] for k in range(len(v) - 1)]
    d, z0, z1, z2 = [None], [None], [None], [None]
    for k in range(1, len(v) - 1):
        dk = e[k] - e[k - 1]
        mid = e[k] + e[k - 1]
        square = dk * dk
        flat = mid * mid + 4e-6
        s1 = flat + (13.0 / 3.0) * square
        both = flat + (25.0 / 3.0) * square
        cross = (4.0 * dk) * mid
        s0, s2 = both + cross, both - cross
        d.append(dk)
        z0.append(s0 * s0)
        z1.append(s1 * s1)
        z2.append(s2 * s2)
    return d, z0, z1, z2


def correction(z0, z1, z2, d0, d1, d2):
    w0, w1, w2 = 1.0 / z0, 2.0 / z1, 1.0 / z2
    top = w0 * ((2.0 / 3.0) * d0 - d1) - (w1 * d1 + w2 * d2)
    return top * (1.0 / (w0 + 3.0 * (w1 + w2)))


def weno(fpm, oh, n, tile):
    layers = FINE + 6
    fp = [fpm[(n, k) + tile] for k in range(layers)]
    fm = [fpm[(5 + n, k) + tile] for k in range(layers)]
    dp, p0, p1, p2 = cell_terms(fp)
    dm, m0, m1, m2 = cell_terms(fm)
    last = None
    for k in range(2, layers - 3):
        face = (fp[k] + fm[k]) + (fp[k + 1] + fm[k + 1])
        face = face + correction(p0[k - 1], p1[k], p2[k + 1], dp[k - 1], dp[k], dp[k + 1])
        face = face + correction(m2[k + 2], m1[k + 1], m0[k], dm[k + 2], dm[k + 1], dm[k])
        if last is not None:
            oh[(n, k - 3) + tile] = last - face
        last = face


def iota2(shape, dim):
    return lax.broadcasted_iota(jnp.int32, shape, dim)


def refine_weights(fine_pos, coarse_pos, start):
    center = start + (fine_pos >> 1)
    side = center + 2 * (fine_pos & 1) - 1
    return jnp.where(coarse_pos == center, 0.75, jnp.where(coarse_pos == side, 0.25, 0.0)).astype(F32)


def thirds(v):
    high = v.astype(jnp.bfloat16)
    rest = v - high.astype(F32)
    mid = rest.astype(jnp.bfloat16)
    low = (rest - mid.astype(F32)).astype(jnp.bfloat16)
    return [high, mid, low]


def times(v, weights):
    return jnp.dot(jnp.concatenate(thirds(v), 1), weights, preferred_element_type=F32)


def applied(weights, v):
    return jnp.dot(weights, jnp.concatenate(thirds(v), 0), preferred_element_type=F32)


def make_fine(mp, fine, py, pz, layers):
    for m, f in enumerate((LAPSE, SHIFT, CONF)):
        coarse = jnp.concatenate([mp[f, 1 + t] for t in layers], 0)
        wide = times(coarse, pz[...])
        for part in range(0, len(layers), 4):
            block = applied(py[...], wide[CY * part : CY * (part + 4)])
            for k in range(4):
                fine[m, layers[part + k]] = block[CY * k : CY * (k + 1)]


def make_sources(fl, vyz, summed, src, plane, ry, rz):
    def pair(c, _):
        cells = []
        for s in range(2):
            j = 2 * c + s
            q = j + 3
            dot = fl[1, q] * fl[5, q] + fl[2, q] * vyz[0, j] + fl[3, q] * vyz[1, j]
            cells.append(fl[4, q] + fl[0, q] + dot + 3.0 * fl[6, q])
        summed[c] = cells[0] + cells[1]
        return 0

    lax.fori_loop(0, COARSE, pair, 0)
    level = times(summed[...].reshape(COARSE * CY, CZ), rz[...])
    level = applied(ry[...], level).reshape(COARSE, CY, CZ)
    src[1:COARSE] = level[: COARSE - 1]
    plane[...] = pltpu.roll(level[COARSE - 1], CZ - CZ // 4, 1)[CY // 4 : CY // 4 + CY // 2, : CZ // 2]


def kernel(sizes, lapse, conf, curv, metric, trace, shift, dens, mom, ener, vel, pres, ob, oh, mp, src,
           fl, vyz, plane, summed, dd, fine, fpm, py, pz, ry, rz, ysten, zsten, lsem, ssem, rsem):
    stars, blocks = sizes
    count = stars * blocks
    blk = lax.axis_index("blk")
    me = lax.axis_index("star") * blocks + blk
    up = lax.rem(me + 1, count)
    down = lax.rem(me + count - 1, count)
    up = (up // blocks, lax.rem(up, blocks))
    down = (down // blocks, lax.rem(down, blocks))

    barrier = pltpu.get_barrier_semaphore()
    for device in (up, down):
        pl.semaphore_signal(barrier, inc=1, device_id=device, device_id_type=MESH)

    own = pl.ds(2, COARSE)
    fown = pl.ds(3, FINE)
    loads = [
        pltpu.make_async_copy(source, target, lsem.at[k])
        for k, (source, target) in enumerate((
            (dens.at[0], fl.at[0, fown]),
            (mom.at[0], fl.at[pl.ds(1, 3), fown]),
            (ener.at[0], fl.at[4, fown]),
            (vel.at[0, 0], fl.at[5, fown]),
            (pres.at[0], fl.at[6, fown]),
            (vel.at[0, pl.ds(1, 2)], vyz),
            (shift, mp.at[pl.ds(SHIFT, 3), own]),
            (lapse, mp.at[LAPSE, own]),
            (conf, mp.at[CONF, own]),
            (curv, mp.at[CURV, own]),
            (metric, mp.at[pl.ds(METRIC, 6), own]),
            (trace, mp.at[pl.ds(TRACE, 6), own]),
        ))
    ]
    def tile_at(t):
        return (pl.ds(pl.multiple_of((t >> 1) * 8, 8), 8), pl.ds(pl.multiple_of((t & 1) * LANES, LANES), LANES))

    def metric_layers(start, inner):
        derivatives(mp, ob, dd, src, ysten, zsten, start, inner)

        def pair(q, _):
            slot, y = q >> 1, q & 1
            for z in range(CZ // LANES):
                tile = (pl.ds(pl.multiple_of(8 * y, 8), 8), pl.ds(LANES * z, LANES))
                rates(mp, ob, dd, slot, start + slot, tile)
            return 0

        lax.fori_loop(0, 4, pair, 0)

    def inner(k, _):
        metric_layers(2 + 2 * k, True)
        return 0

    def first_part():
        for copy in loads:
            copy.start()

        def fill(ref, weights, shape, copies=3):
            part = weights(iota2(shape, 0), iota2(shape, 1)).astype(jnp.bfloat16)
            wide = ref.shape[1] != shape[1]
            for k in range(copies):
                if wide:
                    ref[:, shape[1] * k : shape[1] * k + shape[1]] = part
                else:
                    ref[shape[0] * k : shape[0] * k + shape[0], :] = part

        def in_block(r, c, weights):
            return jnp.where((r ^ c) < CY, weights, 0.0)

        fill(rz, lambda r, c: jnp.where(CZ // 4 + (r >> 1) == c, 0.125, 0.0), (CZ, CZ))
        fill(ry, lambda r, c: in_block(r, c, jnp.where(CY // 4 + ((c & CY - 1) >> 1) == (r & CY - 1), 1.0, 0.0)), (COARSE * CY, COARSE * CY))
        fill(zsten, lambda r, c: stencil(c, r, CZ), (CZ, CZ), 2)
        fill(ysten, lambda r, c: stencil(r, c, CY), (CY, CY), 2)
        fill(pz, lambda r, c: refine_weights(c, r, CZ // 4), (CZ, CZ))
        fill(py, lambda r, c: in_block(r, c, refine_weights(r & CY - 1, c & CY - 1, CY // 4)), (4 * CY, 4 * CY))

        for copy in loads[:6]:
            copy.wait()
        make_sources(fl, vyz, summed, src, plane, ry, rz)
        for copy in loads[6:9]:
            copy.wait()
        make_fine(mp, fine, py, pz, tuple(range(1, 1 + COARSE)))

        def flux_own(jj, _):
            split_flux(fl, fine, fpm, jj)
            return 0

        lax.fori_loop(3, FINE, flux_own, 0)

    def second_part():
        for copy in loads[9:]:
            copy.wait()
        lax.fori_loop(0, COARSE // 2 - 2, inner, 0)

    early = lax.rem(me, max(2, count // 16)) == 0

    @pl.when(early)
    def _():
        first_part()
        second_part()

    pl.semaphore_wait(barrier, 2)

    sends = []

    def send(source, target, device, when=None):
        k = len(sends)
        copy = pltpu.make_async_remote_copy(
            src_ref=source, dst_ref=target, send_sem=ssem.at[k], recv_sem=rsem.at[k], device_id=device, device_id_type=MESH
        )
        sends.append(copy)
        if when is None:
            copy.start()
        else:
            pl.when(when)(copy.start)
        return copy

    starts, ends = blk == 0, blk == blocks - 1
    continues_down, continues_up = jnp.logical_not(starts), jnp.logical_not(ends)

    top, bottom = pl.ds(COARSE - 2, 2), pl.ds(0, 2)
    low, high = pl.ds(0, 2), pl.ds(COARSE + 2, 2)
    bottom3, high3 = pl.ds(0, 3), pl.ds(COARSE + 2, 3)
    ftop, flow, fhigh = pl.ds(FINE - 3, 3), pl.ds(0, 3), pl.ds(FINE + 3, 2)
    first = [
        send(shift.at[:, top], mp.at[pl.ds(SHIFT, 3), low], up),
        send(shift.at[0, bottom3], mp.at[SHIFT, high3], down),
        send(shift.at[pl.ds(1, 2), bottom], mp.at[pl.ds(SHIFT + 1, 2), high], down),
        send(lapse.at[top], mp.at[LAPSE, low], up),
        send(lapse.at[bottom3], mp.at[LAPSE, high3], down),
        send(conf.at[top], mp.at[CONF, low], up),
        send(conf.at[bottom3], mp.at[CONF, high3], down),
    ]
    from_below, from_above = [], []
    for source, target in (
        (lambda s: dens.at[0, s], lambda s: fl.at[0, s]),
        (lambda s: mom.at[0, :, s], lambda s: fl.at[pl.ds(1, 3), s]),
        (lambda s: ener.at[0, s], lambda s: fl.at[4, s]),
        (lambda s: vel.at[0, 0, s], lambda s: fl.at[5, s]),
        (lambda s: pres.at[0, s], lambda s: fl.at[6, s]),
    ):
        from_below.append(send(source(ftop), target(flow), up, continues_up))
        from_above.append(send(source(bottom), target(fhigh), down, continues_down))

    pl.when(jnp.logical_not(early))(first_part)
    from_above.append(send(fpm.at[pl.ds(5, 5), 5], fpm.at[pl.ds(5, 5), FINE + 5], down, continues_down))
    third = [send(plane, src.at[0, pl.ds(0, CY // 2), pl.ds(0, CZ // 2)], up)]
    third += [
        send(curv.at[top], mp.at[CURV, low], up),
        send(curv.at[bottom], mp.at[CURV, high], down),
        send(metric.at[:, top], mp.at[pl.ds(METRIC, 6), low], up),
        send(metric.at[:, bottom], mp.at[pl.ds(METRIC, 6), high], down),
        send(trace.at[:, top], mp.at[pl.ds(TRACE, 6), low], up),
        send(trace.at[:, bottom], mp.at[pl.ds(TRACE, 6), high], down),
    ]
    pl.when(jnp.logical_not(early))(second_part)

    def outer(k, _):
        metric_layers(k * (COARSE - 2), False)
        return 0

    for copy in first:
        copy.wait_recv()
    lax.fori_loop(0, 2, outer, 0)
    make_fine(mp, fine, py, pz, (0, 1 + COARSE, 2 + COARSE, 3 + COARSE))
    for jj in range(FINE, FINE + 3):
        split_flux(fl, fine, fpm, jj)

    @pl.when(continues_down)
    def _():
        for copy in from_below:
            copy.wait_recv()
        for jj in range(3):
            split_flux(fl, fine, fpm, jj)

    @pl.when(starts)
    def _():
        fpm[:, :3] = jnp.zeros((10, 3, CY, CZ), F32)

    @pl.when(continues_up)
    def _():
        for copy in from_above:
            copy.wait_recv()
        for jj in range(FINE + 3, FINE + 5):
            split_flux(fl, fine, fpm, jj)

    @pl.when(ends)
    def _():
        fpm[:, FINE + 3 :] = jnp.zeros((10, 3, CY, CZ), F32)

    def faces(q, _):
        weno(fpm, oh, q >> 2, tile_at(q & 3))
        return 0

    lax.fori_loop(0, 20, faces, 0)

    for copy in first:
        copy.wait_send()

    @pl.when(continues_up)
    def _():
        for copy in from_below:
            copy.wait_send()

    @pl.when(continues_down)
    def _():
        for copy in from_above:
            copy.wait_send()

    for copy in third:
        copy.wait_recv()
    for copy in third:
        copy.wait_send()


def write_out(pb, ph, mp, src, ob, oh, edge, sem):
    copies = []

    def put(source, target):
        copy = pltpu.make_async_copy(source, target, sem.at[len(copies)])
        copy.start()
        copies.append(copy)

    rest = SHIFT - CURV
    middle = pl.ds(2, COARSE - 4)
    put(pb.at[pl.ds(CURV, rest), middle], ob.at[pl.ds(CURV, rest), middle])
    put(ph, oh.at[0])
    put(pb.at[pl.ds(0, CURV)], ob.at[pl.ds(0, CURV)])
    for k, i in enumerate((0, 1, COARSE - 2, COARSE - 1)):
        r = i + 2
        bx12 = mp[SHIFT, r] * (1.0 / 12.0)
        for f in range(CURV, SHIFT):
            moved = bx12 * x_first(mp, f, r)
            if f == CURV:
                source = src[i]
                if i == 0:
                    source = jnp.concatenate([source[: CY // 2, : CZ // 2], jnp.zeros((CY // 2, CZ // 2), F32)], 1)
                    around = jnp.zeros((CY // 4, CZ), F32)
                    source = jnp.concatenate([around, pltpu.roll(source, CZ // 4, 1), around], 0)
                moved = moved + (4.0 * math.pi) * mp[LAPSE, r] * source
            edge[f - CURV, k] = pb[f, i] + moved
        if k % 2:
            put(edge.at[:, pl.ds(k - 1, 2)], ob.at[pl.ds(CURV, rest), pl.ds(i - 1, 2)])
    for copy in copies:
        copy.wait()


def on_device(sizes, *arrays):
    hbm = pl.BlockSpec(memory_space=pltpu.HBM)
    vmem = pl.BlockSpec(memory_space=pltpu.VMEM)
    metric_out, fluid_out = (15, COARSE, CY, CZ), (5, FINE, CY, CZ)
    part = pl.pallas_call(
        functools.partial(kernel, sizes),
        out_shape=(
            pltpu.VMEM(metric_out, F32),
            pltpu.VMEM(fluid_out, F32),
            pltpu.VMEM((18, COARSE + 5, CY, CZ), F32),
            pltpu.VMEM((COARSE, CY, CZ), F32),
        ),
        in_specs=[hbm] * 11,
        out_specs=(vmem,) * 4,
        scratch_shapes=[
            pltpu.VMEM((7, FINE + 6, CY, CZ), F32),
            pltpu.VMEM((2, FINE, CY, CZ), F32),
            pltpu.VMEM((CY // 2, CZ // 2), F32),
            pltpu.VMEM((COARSE, CY, CZ), F32),
            pltpu.VMEM((2, 15, CY, CZ), F32),
            pltpu.VMEM((3, 12, CY, CZ), F32),
            pltpu.VMEM((10, FINE + 6, CY, CZ), F32),
            pltpu.VMEM((4 * CY, 3 * 4 * CY), jnp.bfloat16),
            pltpu.VMEM((3 * CZ, CZ), jnp.bfloat16),
            pltpu.VMEM((COARSE * CY, 3 * COARSE * CY), jnp.bfloat16),
            pltpu.VMEM((3 * CZ, CZ), jnp.bfloat16),
            pltpu.VMEM((CY, 2 * CY), jnp.bfloat16),
            pltpu.VMEM((2 * CZ, CZ), jnp.bfloat16),
            pltpu.SemaphoreType.DMA((12,)),
            pltpu.SemaphoreType.DMA((25,)),
            pltpu.SemaphoreType.DMA((25,)),
        ],
        compiler_params=pltpu.CompilerParams(collective_id=0, has_side_effects=True, vmem_limit_bytes=54 << 20),
        cost_estimate=pl.CostEstimate(flops=60_000_000, bytes_accessed=8_000_000, transcendentals=0),
    )(*arrays)
    anywhere = pl.BlockSpec(memory_space=pl.ANY)
    return pl.pallas_call(
        write_out,
        out_shape=(jax.ShapeDtypeStruct(metric_out, F32), jax.ShapeDtypeStruct((1,) + fluid_out, F32)),
        in_specs=[vmem] * 4,
        out_specs=(anywhere, anywhere),
        scratch_shapes=[pltpu.VMEM((SHIFT - CURV, 4, CY, CZ), F32), pltpu.SemaphoreType.DMA((5,))],
        compiler_params=pltpu.CompilerParams(vmem_limit_bytes=16 << 20),
        cost_estimate=pl.CostEstimate(flops=0, bytes_accessed=6_400_000, transcendentals=0),
    )(*part)


def solution(mesh):
    level = P(("star", "blk"), None, None)
    level4 = P(None, ("star", "blk"), None, None)
    box = P("star", "blk", None, None)
    box5 = P("star", None, "blk", None, None)
    sizes = (mesh.shape["star"], mesh.shape["blk"])
    return jax.shard_map(
        functools.partial(on_device, sizes),
        mesh=mesh,
        in_specs=(level, level, level, level4, level4, level4, box, box5, box, box5, box),
        out_specs=(level4, box5),
        check_vma=False,
    )
```

```python
import functools
import math

import jax
import jax.numpy as jnp
from jax import lax
from jax.experimental import pallas as pl
from jax.experimental.pallas import tpu as pltpu
from jax.sharding import PartitionSpec as P

MESH = pl.DeviceIdType.MESH
F32 = jnp.float32

pair_index = ((0, 1, 2), (1, 3, 4), (2, 4, 5))
sym_pairs = ((0, 0), (0, 1), (0, 2), (1, 1), (1, 2), (2, 2))

LAPSE, CONF, CURV, METRIC, TRACE, SHIFT = 0, 1, 2, 3, 9, 15
COARSE, FINE = 8, 16
CY, CZ = 16, 256
LANES = 128


def total(terms):
    return functools.reduce(lambda x, y: x + y, terms)


def rolled(v, axis):
    n = v.shape[axis]
    if axis == 1:
        return [pltpu.roll(v, s, 1) for s in (2, 1, n - 1, n - 2)]
    low, high = v[:8], v[8:]
    row = iota2(low.shape, 0)
    out = []
    for s in (2, 1, 7, 6):
        a, b = pltpu.roll(low, s, 0), pltpu.roll(high, s, 0)
        wrapped = row < s
        if s < 4:
            parts = [jnp.where(wrapped, b, a), jnp.where(wrapped, a, b)]
        else:
            parts = [jnp.where(wrapped, a, b), jnp.where(wrapped, b, a)]
        out.append(jnp.concatenate(parts, 0))
    return out


def halves(v):
    high = v.astype(jnp.bfloat16)
    return [high, (v - high.astype(F32)).astype(jnp.bfloat16)]


def stencil(to, source, n):
    ahead = (source - to) & (n - 1)
    near = jnp.where(ahead == 1, 8.0, jnp.where(ahead == n - 1, -8.0, 0.0))
    return jnp.where(ahead == 2, -1.0, jnp.where(ahead == n - 2, 1.0, near))


def first_of(moved):
    return (moved[0] - moved[3]) + 8.0 * (moved[2] - moved[1])


def second_of(v, moved):
    return 16.0 * (moved[1] + moved[2]) - (moved[0] + moved[3]) - 30.0 * v


def ring_first(v, axis):
    return first_of(rolled(v, axis))


def x_first(mp, f, r):
    return (mp[f, r - 2] - mp[f, r + 2]) + 8.0 * (mp[f, r + 1] - mp[f, r - 1])


def derivatives(mp, ob, dd, src, ysten, zsten, start, inner):
    fields = range(1, SHIFT + 3)
    layers = [start, start + 1]
    parts = [[halves(mp[f, i + 2]) for f in fields] for i in layers]
    flat = jnp.concatenate([jnp.concatenate(p, 1) for layer in parts for p in layer], 0)
    flat = jnp.dot(flat, zsten[...], preferred_element_type=F32)
    for slot, i in enumerate(layers):
        r = i + 2
        bx12, by12, bz12 = [mp[SHIFT + k, r] * (1.0 / 12.0) for k in range(3)]
        base = len(fields) * slot - 1
        dz = {f: flat[CY * (base + f) : CY * (base + f + 1)] for f in fields}
        dy = {f: jnp.dot(ysten[...], jnp.concatenate(parts[slot][f - 1], 0), preferred_element_type=F32) for f in fields}

        v = mp[LAPSE, r]
        along = x_first(mp, LAPSE, r)
        ys, zs = rolled(v, 0), rolled(v, 1)
        lapse_z = first_of(zs)
        ob[LAPSE, i] = bx12 * along + by12 * first_of(ys) + bz12 * lapse_z
        outer = (mp[LAPSE, r - 2] + mp[LAPSE, r + 2]) + 30.0 * v
        dd[slot, 9] = (16.0 * (mp[LAPSE, r - 1] + mp[LAPSE, r + 1]) - outer) * (1.0 / 12.0)
        dd[slot, 10] = ring_first(along, 0) * (1.0 / 144.0)
        dd[slot, 11] = ring_first(along, 1) * (1.0 / 144.0)
        dd[slot, 12] = second_of(v, ys) * (1.0 / 12.0)
        dd[slot, 13] = ring_first(lapse_z, 0) * (1.0 / 144.0)
        dd[slot, 14] = second_of(v, zs) * (1.0 / 12.0)
        for f in range(1, SHIFT):
            moved = by12 * dy[f] + bz12 * dz[f]
            if inner or f == CONF:
                moved = moved + bx12 * x_first(mp, f, r)
            if inner and f == CURV:
                moved = moved + (4.0 * math.pi) * v * src[i]
            ob[f, i] = moved
        for k in range(3):
            dd[slot, k] = x_first(mp, SHIFT + k, r) * (1.0 / 12.0)
            dd[slot, 3 + k] = dy[SHIFT + k] * (1.0 / 12.0)
            dd[slot, 6 + k] = dz[SHIFT + k] * (1.0 / 12.0)


def rates(mp, ob, dd, slot, i, tile):
    r = i + 2
    al, ch, kk = [mp[(f, r) + tile] for f in (LAPSE, CONF, CURV)]
    g = [mp[(METRIC + p, r) + tile] for p in range(6)]
    ds = [[dd[(slot, 3 * k + j) + tile] for j in range(3)] for k in range(3)]
    hess = [dd[(slot, 9 + p) + tile] for p in range(6)]
    div = ds[0][0] + ds[1][1] + ds[2][2]
    tdiv = div * (2.0 / 3.0)
    a, b, c, d, e, f = g
    cof = (d * f - e * e, c * e - b * f, b * e - c * d, a * f - c * c, b * c - a * e, a * d - b * b)
    rdet = 1.0 / (a * cof[0] + b * cof[1] + c * cof[2])
    inv = [entry * rdet for entry in cof]
    alk = al * kk
    al2 = 2.0 * al
    ob[(0, i) + tile] = ob[(0, i) + tile] - 2.0 * alk
    ob[(1, i) + tile] = ob[(1, i) + tile] + (2.0 / 3.0) * ch * (alk - div)
    trh = (inv[0] * hess[0] + inv[3] * hess[3] + inv[5] * hess[5]) + 2.0 * (inv[1] * hess[1] + inv[2] * hess[2] + inv[4] * hess[4])
    cv = [mp[(TRACE + p, r) + tile] for p in range(6)]
    mixed = [[total([cv[pair_index[p][k]] * inv[pair_index[k][q]] for k in range(3)]) for q in range(3)] for p in range(3)]
    square = (mixed[0][0] * mixed[0][0] + mixed[1][1] * mixed[1][1] + mixed[2][2] * mixed[2][2]) + 2.0 * (
        mixed[0][1] * mixed[1][0] + mixed[0][2] * mixed[2][0] + mixed[1][2] * mixed[2][1]
    )
    chtr = ch * trh
    ob[(2, i) + tile] = ob[(2, i) + tile] - chtr + al * (square + kk * kk * (1.0 / 3.0))
    chtr3 = chtr * (1.0 / 3.0)
    scale = alk - tdiv
    for p, (x, y) in enumerate(sym_pairs):
        if x == y:
            moved_g = 2.0 * total([g[pair_index[x][k]] * ds[x][k] for k in range(3)])
            moved_c = 2.0 * total([cv[pair_index[x][k]] * ds[x][k] for k in range(3)])
        else:
            moved_g = total([g[pair_index[x][k]] * ds[y][k] + g[pair_index[y][k]] * ds[x][k] for k in range(3)])
            moved_c = total([cv[pair_index[x][k]] * ds[y][k] + cv[pair_index[y][k]] * ds[x][k] for k in range(3)])
        ob[(3 + p, i) + tile] = ob[(3 + p, i) + tile] - al2 * cv[p] + moved_g - tdiv * g[p]
        product = total([mixed[x][k] * cv[pair_index[k][y]] for k in range(3)])
        ob[(9 + p, i) + tile] = ob[(9 + p, i) + tile] + scale * cv[p] - al2 * product + moved_c - ch * hess[p] + chtr3 * g[p]


def motion(fl, fine, jj):
    odd = jj & 1
    t = (jj + 1) >> 1
    u = t + 1 - 2 * odd
    lapse, shift, conf = [0.75 * fine[m, t] + 0.25 * fine[m, u] for m in range(3)]
    root = lax.rsqrt(conf)
    return lapse * fl[5, jj] - shift, lapse + jnp.abs(shift), lapse * (root * root * root) * fl[6, jj]


def split_flux(fl, fine, fpm, jj, given=None):
    moved, speed, weight = motion(fl, fine, jj) if given is None else given
    vel = fl[5, jj]
    plus = 0.5 * (moved + speed)
    minus = 0.5 * (moved - speed)
    half = 0.5 * weight
    extra = (None, half, None, None, half * vel)
    for n in range(5):
        v = fl[n, jj]
        fp, fm = v * plus, v * minus
        if extra[n] is not None:
            fp, fm = fp + extra[n], fm + extra[n]
        fpm[n, jj] = fp
        fpm[5 + n, jj] = fm


def cell_terms(v):
    e = [v[k + 1] - v[k] for k in range(len(v) - 1)]
    d, z0, z1, z2 = [None], [None], [None], [None]
    for k in range(1, len(v) - 1):
        dk = e[k] - e[k - 1]
        mid = e[k] + e[k - 1]
        square = dk * dk
        flat = mid * mid + 4e-6
        s1 = flat + (13.0 / 3.0) * square
        both = flat + (25.0 / 3.0) * square
        cross = (4.0 * dk) * mid
        s0, s2 = both + cross, both - cross
        d.append(dk)
        z0.append(s0 * s0)
        z1.append(s1 * s1)
        z2.append(s2 * s2)
    return d, z0, z1, z2


def correction(z0, z1, z2, d0, d1, d2):
    w0, w1, w2 = 1.0 / z0, 2.0 / z1, 1.0 / z2
    top = w0 * ((2.0 / 3.0) * d0 - d1) - (w1 * d1 + w2 * d2)
    return top * (1.0 / (w0 + 3.0 * (w1 + w2)))


def weno(fpm, oh, n, tile):
    layers = FINE + 6
    fp = [fpm[(n, k) + tile] for k in range(layers)]
    fm = [fpm[(5 + n, k) + tile] for k in range(layers)]
    dp, p0, p1, p2 = cell_terms(fp)
    dm, m0, m1, m2 = cell_terms(fm)
    last = None
    for k in range(2, layers - 3):
        face = (fp[k] + fm[k]) + (fp[k + 1] + fm[k + 1])
        face = face + correction(p0[k - 1], p1[k], p2[k + 1], dp[k - 1], dp[k], dp[k + 1])
        face = face + correction(m2[k + 2], m1[k + 1], m0[k], dm[k + 2], dm[k + 1], dm[k])
        if last is not None:
            oh[(n, k - 3) + tile] = last - face
        last = face


def iota2(shape, dim):
    return lax.broadcasted_iota(jnp.int32, shape, dim)


def refine_weights(fine_pos, coarse_pos, start):
    center = start + (fine_pos >> 1)
    side = center + 2 * (fine_pos & 1) - 1
    return jnp.where(coarse_pos == center, 0.75, jnp.where(coarse_pos == side, 0.25, 0.0)).astype(F32)


def thirds(v):
    high = v.astype(jnp.bfloat16)
    rest = v - high.astype(F32)
    mid = rest.astype(jnp.bfloat16)
    low = (rest - mid.astype(F32)).astype(jnp.bfloat16)
    return [high, mid, low]


def times(v, weights):
    return jnp.dot(jnp.concatenate(thirds(v), 1), weights, preferred_element_type=F32)


def applied(weights, v):
    return jnp.dot(weights, jnp.concatenate(thirds(v), 0), preferred_element_type=F32)


def make_fine(mp, fine, py, pz, layers):
    for m, f in enumerate((LAPSE, SHIFT, CONF)):
        coarse = jnp.concatenate([mp[f, 1 + t] for t in layers], 0)
        wide = times(coarse, pz[...])
        for part in range(0, len(layers), 4):
            block = applied(py[...], wide[CY * part : CY * (part + 4)])
            for k in range(4):
                fine[m, layers[part + k]] = block[CY * k : CY * (k + 1)]


def make_sources(fl, vyz, summed, src, plane, ry, rz):
    def pair(c, _):
        cells = []
        for s in range(2):
            j = 2 * c + s
            q = j + 3
            dot = fl[1, q] * fl[5, q] + fl[2, q] * vyz[0, j] + fl[3, q] * vyz[1, j]
            cells.append(fl[4, q] + fl[0, q] + dot + 3.0 * fl[6, q])
        summed[c] = cells[0] + cells[1]
        return 0

    lax.fori_loop(0, COARSE, pair, 0)
    level = times(summed[...].reshape(COARSE * CY, CZ), rz[...])
    level = applied(ry[...], level).reshape(COARSE, CY, CZ)
    src[1:COARSE] = level[: COARSE - 1]
    plane[...] = pltpu.roll(level[COARSE - 1], CZ - CZ // 4, 1)[CY // 4 : CY // 4 + CY // 2, : CZ // 2]


def kernel(sizes, lapse, conf, curv, metric, trace, shift, dens, mom, ener, vel, pres, ob, oh, mp, src,
           fl, vyz, plane, summed, dd, fine, fpm, py, pz, ry, rz, ysten, zsten, drift, lsem, ssem, rsem):
    stars, blocks = sizes
    count = stars * blocks
    blk = lax.axis_index("blk")
    me = lax.axis_index("star") * blocks + blk
    up = lax.rem(me + 1, count)
    down = lax.rem(me + count - 1, count)
    up = (up // blocks, lax.rem(up, blocks))
    down = (down // blocks, lax.rem(down, blocks))

    barrier = pltpu.get_barrier_semaphore()
    for device in (up, down):
        pl.semaphore_signal(barrier, inc=1, device_id=device, device_id_type=MESH)

    own = pl.ds(2, COARSE)
    fown = pl.ds(3, FINE)
    loads = [
        pltpu.make_async_copy(source, target, lsem.at[k])
        for k, (source, target) in enumerate((
            (dens.at[0], fl.at[0, fown]),
            (mom.at[0], fl.at[pl.ds(1, 3), fown]),
            (ener.at[0], fl.at[4, fown]),
            (vel.at[0, 0], fl.at[5, fown]),
            (pres.at[0], fl.at[6, fown]),
            (vel.at[0, pl.ds(1, 2)], vyz),
            (shift, mp.at[pl.ds(SHIFT, 3), own]),
            (lapse, mp.at[LAPSE, own]),
            (conf, mp.at[CONF, own]),
            (curv, mp.at[CURV, own]),
            (metric, mp.at[pl.ds(METRIC, 6), own]),
            (trace, mp.at[pl.ds(TRACE, 6), own]),
        ))
    ]
    def tile_at(t):
        return (pl.ds(pl.multiple_of((t >> 1) * 8, 8), 8), pl.ds(pl.multiple_of((t & 1) * LANES, LANES), LANES))

    def metric_layers(start, inner):
        derivatives(mp, ob, dd, src, ysten, zsten, start, inner)

        def pair(q, _):
            slot, y = q >> 1, q & 1
            for z in range(CZ // LANES):
                tile = (pl.ds(pl.multiple_of(8 * y, 8), 8), pl.ds(LANES * z, LANES))
                rates(mp, ob, dd, slot, start + slot, tile)
            return 0

        lax.fori_loop(0, 4, pair, 0)

    def inner(k, _):
        metric_layers(2 + 2 * k, True)
        return 0

    def first_part():
        for copy in loads:
            copy.start()

        def fill(ref, weights, shape, copies=3):
            part = weights(iota2(shape, 0), iota2(shape, 1)).astype(jnp.bfloat16)
            wide = ref.shape[1] != shape[1]
            for k in range(copies):
                if wide:
                    ref[:, shape[1] * k : shape[1] * k + shape[1]] = part
                else:
                    ref[shape[0] * k : shape[0] * k + shape[0], :] = part

        def in_block(r, c, weights):
            return jnp.where((r ^ c) < CY, weights, 0.0)

        fill(rz, lambda r, c: jnp.where(CZ // 4 + (r >> 1) == c, 0.125, 0.0), (CZ, CZ))
        fill(ry, lambda r, c: in_block(r, c, jnp.where(CY // 4 + ((c & CY - 1) >> 1) == (r & CY - 1), 1.0, 0.0)), (COARSE * CY, COARSE * CY))
        fill(zsten, lambda r, c: stencil(c, r, CZ), (CZ, CZ), 2)
        fill(ysten, lambda r, c: stencil(r, c, CY), (CY, CY), 2)
        fill(pz, lambda r, c: refine_weights(c, r, CZ // 4), (CZ, CZ))
        fill(py, lambda r, c: in_block(r, c, refine_weights(r & CY - 1, c & CY - 1, CY // 4)), (4 * CY, 4 * CY))

        for copy in loads[:6]:
            copy.wait()
        make_sources(fl, vyz, summed, src, plane, ry, rz)
        for copy in loads[6:9]:
            copy.wait()
        make_fine(mp, fine, py, pz, tuple(range(1, 1 + COARSE)))

        def flux_own(jj, _):
            split_flux(fl, fine, fpm, jj)
            return 0

        lax.fori_loop(3, FINE, flux_own, 0)
        for k, value in enumerate(motion(fl, fine, 4)):
            drift[0, k] = value

    def second_part():
        for copy in loads[9:]:
            copy.wait()
        lax.fori_loop(0, COARSE // 2 - 2, inner, 0)

    early = lax.rem(me, max(2, count // 16)) == 0

    @pl.when(early)
    def _():
        first_part()
        second_part()

    pl.semaphore_wait(barrier, 2)

    sends = []

    def send(source, target, device, when=None):
        k = len(sends)
        copy = pltpu.make_async_remote_copy(
            src_ref=source, dst_ref=target, send_sem=ssem.at[k], recv_sem=rsem.at[k], device_id=device, device_id_type=MESH
        )
        sends.append(copy)
        if when is None:
            copy.start()
        else:
            pl.when(when)(copy.start)
        return copy

    starts, ends = blk == 0, blk == blocks - 1
    continues_down, continues_up = jnp.logical_not(starts), jnp.logical_not(ends)

    top, bottom = pl.ds(COARSE - 2, 2), pl.ds(0, 2)
    low, high = pl.ds(0, 2), pl.ds(COARSE + 2, 2)
    ftop, flow, fhigh = pl.ds(FINE - 3, 3), pl.ds(0, 3), pl.ds(FINE + 3, 2)
    first = [
        send(shift.at[:, top], mp.at[pl.ds(SHIFT, 3), low], up),
        send(shift.at[:, bottom], mp.at[pl.ds(SHIFT, 3), high], down),
        send(lapse.at[top], mp.at[LAPSE, low], up),
        send(lapse.at[bottom], mp.at[LAPSE, high], down),
        send(conf.at[top], mp.at[CONF, low], up),
        send(conf.at[bottom], mp.at[CONF, high], down),
    ]
    from_below, from_above = [], []
    pressure = lambda s: pres.at[0, s]
    for source, target in (
        (lambda s: dens.at[0, s], lambda s: fl.at[0, s]),
        (lambda s: mom.at[0, :, s], lambda s: fl.at[pl.ds(1, 3), s]),
        (lambda s: ener.at[0, s], lambda s: fl.at[4, s]),
        (lambda s: vel.at[0, 0, s], lambda s: fl.at[5, s]),
        (pressure, lambda s: fl.at[6, s]),
    ):
        from_below.append(send(source(ftop), target(flow), up, continues_up))
        if source is pressure:
            from_above.append(send(pres.at[0, pl.ds(0, 1)], fl.at[6, pl.ds(FINE + 3, 1)], down, continues_down))
        else:
            from_above.append(send(source(bottom), target(fhigh), down, continues_down))

    pl.when(jnp.logical_not(early))(first_part)
    from_above.append(send(fpm.at[pl.ds(5, 5), 5], fpm.at[pl.ds(5, 5), FINE + 5], down, continues_down))
    from_above.append(send(drift.at[0], drift.at[1], down, continues_down))
    third = [send(plane, src.at[0, pl.ds(0, CY // 2), pl.ds(0, CZ // 2)], up)]
    third += [
        send(curv.at[top], mp.at[CURV, low], up),
        send(curv.at[bottom], mp.at[CURV, high], down),
        send(metric.at[:, top], mp.at[pl.ds(METRIC, 6), low], up),
        send(metric.at[:, bottom], mp.at[pl.ds(METRIC, 6), high], down),
        send(trace.at[:, top], mp.at[pl.ds(TRACE, 6), low], up),
        send(trace.at[:, bottom], mp.at[pl.ds(TRACE, 6), high], down),
    ]
    pl.when(jnp.logical_not(early))(second_part)

    def outer(k, _):
        metric_layers(k * (COARSE - 2), False)
        return 0

    for copy in first:
        copy.wait_recv()
    lax.fori_loop(0, 2, outer, 0)
    make_fine(mp, fine, py, pz, (0, 1 + COARSE, 2 + COARSE, 2 + COARSE))
    for jj in range(FINE, FINE + 3):
        split_flux(fl, fine, fpm, jj)

    @pl.when(continues_down)
    def _():
        for copy in from_below:
            copy.wait_recv()
        for jj in range(3):
            split_flux(fl, fine, fpm, jj)

    @pl.when(starts)
    def _():
        fpm[:, :3] = jnp.zeros((10, 3, CY, CZ), F32)

    @pl.when(continues_up)
    def _():
        for copy in from_above:
            copy.wait_recv()
        split_flux(fl, fine, fpm, FINE + 3)
        split_flux(fl, fine, fpm, FINE + 4, [drift[1, k] for k in range(3)])

    @pl.when(ends)
    def _():
        fpm[:, FINE + 3 :] = jnp.zeros((10, 3, CY, CZ), F32)

    def faces(q, _):
        weno(fpm, oh, q >> 2, tile_at(q & 3))
        return 0

    lax.fori_loop(0, 20, faces, 0)

    for copy in first:
        copy.wait_send()

    @pl.when(continues_up)
    def _():
        for copy in from_below:
            copy.wait_send()

    @pl.when(continues_down)
    def _():
        for copy in from_above:
            copy.wait_send()

    for copy in third:
        copy.wait_recv()
    for copy in third:
        copy.wait_send()


def write_out(pb, ph, mp, src, ob, oh, edge, sem):
    copies = []

    def put(source, target):
        copy = pltpu.make_async_copy(source, target, sem.at[len(copies)])
        copy.start()
        copies.append(copy)

    rest = SHIFT - CURV
    middle = pl.ds(2, COARSE - 4)
    put(pb.at[pl.ds(CURV, rest), middle], ob.at[pl.ds(CURV, rest), middle])
    put(ph, oh.at[0])
    put(pb.at[pl.ds(0, CURV)], ob.at[pl.ds(0, CURV)])
    for k, i in enumerate((0, 1, COARSE - 2, COARSE - 1)):
        r = i + 2
        bx12 = mp[SHIFT, r] * (1.0 / 12.0)
        for f in range(CURV, SHIFT):
            moved = bx12 * x_first(mp, f, r)
            if f == CURV:
                source = src[i]
                if i == 0:
                    source = jnp.concatenate([source[: CY // 2, : CZ // 2], jnp.zeros((CY // 2, CZ // 2), F32)], 1)
                    around = jnp.zeros((CY // 4, CZ), F32)
                    source = jnp.concatenate([around, pltpu.roll(source, CZ // 4, 1), around], 0)
                moved = moved + (4.0 * math.pi) * mp[LAPSE, r] * source
            edge[f - CURV, k] = pb[f, i] + moved
        if k % 2:
            put(edge.at[:, pl.ds(k - 1, 2)], ob.at[pl.ds(CURV, rest), pl.ds(i - 1, 2)])
    for copy in copies:
        copy.wait()


def on_device(sizes, *arrays):
    hbm = pl.BlockSpec(memory_space=pltpu.HBM)
    vmem = pl.BlockSpec(memory_space=pltpu.VMEM)
    metric_out, fluid_out = (15, COARSE, CY, CZ), (5, FINE, CY, CZ)
    part = pl.pallas_call(
        functools.partial(kernel, sizes),
        out_shape=(
            pltpu.VMEM(metric_out, F32),
            pltpu.VMEM(fluid_out, F32),
            pltpu.VMEM((18, COARSE + 4, CY, CZ), F32),
            pltpu.VMEM((COARSE, CY, CZ), F32),
        ),
        in_specs=[hbm] * 11,
        out_specs=(vmem,) * 4,
        scratch_shapes=[
            pltpu.VMEM((7, FINE + 6, CY, CZ), F32),
            pltpu.VMEM((2, FINE, CY, CZ), F32),
            pltpu.VMEM((CY // 2, CZ // 2), F32),
            pltpu.VMEM((COARSE, CY, CZ), F32),
            pltpu.VMEM((2, 15, CY, CZ), F32),
            pltpu.VMEM((3, 12, CY, CZ), F32),
            pltpu.VMEM((10, FINE + 6, CY, CZ), F32),
            pltpu.VMEM((4 * CY, 3 * 4 * CY), jnp.bfloat16),
            pltpu.VMEM((3 * CZ, CZ), jnp.bfloat16),
            pltpu.VMEM((COARSE * CY, 3 * COARSE * CY), jnp.bfloat16),
            pltpu.VMEM((3 * CZ, CZ), jnp.bfloat16),
            pltpu.VMEM((CY, 2 * CY), jnp.bfloat16),
            pltpu.VMEM((2 * CZ, CZ), jnp.bfloat16),
            pltpu.VMEM((2, 3, CY, CZ), F32),
            pltpu.SemaphoreType.DMA((12,)),
            pltpu.SemaphoreType.DMA((25,)),
            pltpu.SemaphoreType.DMA((25,)),
        ],
        compiler_params=pltpu.CompilerParams(collective_id=0, has_side_effects=True, vmem_limit_bytes=54 << 20),
        cost_estimate=pl.CostEstimate(flops=60_000_000, bytes_accessed=8_000_000, transcendentals=0),
    )(*arrays)
    anywhere = pl.BlockSpec(memory_space=pl.ANY)
    return pl.pallas_call(
        write_out,
        out_shape=(jax.ShapeDtypeStruct(metric_out, F32), jax.ShapeDtypeStruct((1,) + fluid_out, F32)),
        in_specs=[vmem] * 4,
        out_specs=(anywhere, anywhere),
        scratch_shapes=[pltpu.VMEM((SHIFT - CURV, 4, CY, CZ), F32), pltpu.SemaphoreType.DMA((5,))],
        compiler_params=pltpu.CompilerParams(vmem_limit_bytes=16 << 20),
        cost_estimate=pl.CostEstimate(flops=0, bytes_accessed=6_400_000, transcendentals=0),
    )(*part)


def solution(mesh):
    level = P(("star", "blk"), None, None)
    level4 = P(None, ("star", "blk"), None, None)
    box = P("star", "blk", None, None)
    box5 = P("star", None, "blk", None, None)
    sizes = (mesh.shape["star"], mesh.shape["blk"])
    return jax.shard_map(
        functools.partial(on_device, sizes),
        mesh=mesh,
        in_specs=(level, level, level, level4, level4, level4, box, box5, box, box5, box),
        out_specs=(level4, box5),
        check_vma=False,
    )
```

```python
import functools
import math

import jax
import jax.numpy as jnp
from jax import lax
from jax.experimental import pallas as pl
from jax.experimental.pallas import tpu as pltpu
from jax.sharding import PartitionSpec as P

MESH = pl.DeviceIdType.MESH
F32 = jnp.float32

pair_index = ((0, 1, 2), (1, 3, 4), (2, 4, 5))
sym_pairs = ((0, 0), (0, 1), (0, 2), (1, 1), (1, 2), (2, 2))

LAPSE, CONF, CURV, METRIC, TRACE, SHIFT = 0, 1, 2, 3, 9, 15
COARSE, FINE = 8, 16
CY, CZ = 16, 256
LANES = 128


def total(terms):
    return functools.reduce(lambda x, y: x + y, terms)


def rolled(v, axis):
    n = v.shape[axis]
    if axis == 1:
        return [pltpu.roll(v, s, 1) for s in (2, 1, n - 1, n - 2)]
    low, high = v[:8], v[8:]
    row = iota2(low.shape, 0)
    out = []
    for s in (2, 1, 7, 6):
        a, b = pltpu.roll(low, s, 0), pltpu.roll(high, s, 0)
        wrapped = row < s
        if s < 4:
            parts = [jnp.where(wrapped, b, a), jnp.where(wrapped, a, b)]
        else:
            parts = [jnp.where(wrapped, a, b), jnp.where(wrapped, b, a)]
        out.append(jnp.concatenate(parts, 0))
    return out


def halves(v):
    high = v.astype(jnp.bfloat16)
    return [high, (v - high.astype(F32)).astype(jnp.bfloat16)]


def stencil(to, source, n):
    ahead = (source - to) & (n - 1)
    near = jnp.where(ahead == 1, 8.0, jnp.where(ahead == n - 1, -8.0, 0.0))
    return jnp.where(ahead == 2, -1.0, jnp.where(ahead == n - 2, 1.0, near))


def first_of(moved):
    return (moved[0] - moved[3]) + 8.0 * (moved[2] - moved[1])


def second_of(v, moved):
    return 16.0 * (moved[1] + moved[2]) - (moved[0] + moved[3]) - 30.0 * v


def ring_first(v, axis):
    return first_of(rolled(v, axis))


def x_first(mp, f, r):
    return (mp[f, r - 2] - mp[f, r + 2]) + 8.0 * (mp[f, r + 1] - mp[f, r - 1])


def derivatives(mp, ob, dd, src, ysten, zsten, start, inner):
    fields = range(1, SHIFT + 3)
    layers = [start, start + 1]
    parts = [[halves(mp[f, i + 2]) for f in fields] for i in layers]
    flat = jnp.concatenate([jnp.concatenate(p, 1) for layer in parts for p in layer], 0)
    flat = jnp.dot(flat, zsten[...], preferred_element_type=F32)
    for slot, i in enumerate(layers):
        r = i + 2
        bx12, by12, bz12 = [mp[SHIFT + k, r] * (1.0 / 12.0) for k in range(3)]
        base = len(fields) * slot - 1
        dz = {f: flat[CY * (base + f) : CY * (base + f + 1)] for f in fields}
        dy = {f: jnp.dot(ysten[...], jnp.concatenate(parts[slot][f - 1], 0), preferred_element_type=F32) for f in fields}

        v = mp[LAPSE, r]
        along = x_first(mp, LAPSE, r)
        ys, zs = rolled(v, 0), rolled(v, 1)
        lapse_z = first_of(zs)
        ob[LAPSE, i] = bx12 * along + by12 * first_of(ys) + bz12 * lapse_z
        outer = (mp[LAPSE, r - 2] + mp[LAPSE, r + 2]) + 30.0 * v
        dd[slot, 9] = (16.0 * (mp[LAPSE, r - 1] + mp[LAPSE, r + 1]) - outer) * (1.0 / 12.0)
        dd[slot, 10] = ring_first(along, 0) * (1.0 / 144.0)
        dd[slot, 11] = ring_first(along, 1) * (1.0 / 144.0)
        dd[slot, 12] = second_of(v, ys) * (1.0 / 12.0)
        dd[slot, 13] = ring_first(lapse_z, 0) * (1.0 / 144.0)
        dd[slot, 14] = second_of(v, zs) * (1.0 / 12.0)
        for f in range(1, SHIFT):
            moved = by12 * dy[f] + bz12 * dz[f]
            if inner or f == CONF:
                moved = moved + bx12 * x_first(mp, f, r)
            if inner and f == CURV:
                moved = moved + (4.0 * math.pi) * v * src[i]
            ob[f, i] = moved
        for k in range(3):
            dd[slot, k] = x_first(mp, SHIFT + k, r) * (1.0 / 12.0)
            dd[slot, 3 + k] = dy[SHIFT + k] * (1.0 / 12.0)
            dd[slot, 6 + k] = dz[SHIFT + k] * (1.0 / 12.0)


def rates(mp, ob, dd, slot, i, tile):
    r = i + 2
    al, ch, kk = [mp[(f, r) + tile] for f in (LAPSE, CONF, CURV)]
    g = [mp[(METRIC + p, r) + tile] for p in range(6)]
    ds = [[dd[(slot, 3 * k + j) + tile] for j in range(3)] for k in range(3)]
    hess = [dd[(slot, 9 + p) + tile] for p in range(6)]
    div = ds[0][0] + ds[1][1] + ds[2][2]
    tdiv = div * (2.0 / 3.0)
    a, b, c, d, e, f = g
    cof = (d * f - e * e, c * e - b * f, b * e - c * d, a * f - c * c, b * c - a * e, a * d - b * b)
    rdet = 1.0 / (a * cof[0] + b * cof[1] + c * cof[2])
    inv = [entry * rdet for entry in cof]
    alk = al * kk
    al2 = 2.0 * al
    ob[(0, i) + tile] = ob[(0, i) + tile] - 2.0 * alk
    ob[(1, i) + tile] = ob[(1, i) + tile] + (2.0 / 3.0) * ch * (alk - div)
    trh = (inv[0] * hess[0] + inv[3] * hess[3] + inv[5] * hess[5]) + 2.0 * (inv[1] * hess[1] + inv[2] * hess[2] + inv[4] * hess[4])
    cv = [mp[(TRACE + p, r) + tile] for p in range(6)]
    mixed = [[total([cv[pair_index[p][k]] * inv[pair_index[k][q]] for k in range(3)]) for q in range(3)] for p in range(3)]
    square = (mixed[0][0] * mixed[0][0] + mixed[1][1] * mixed[1][1] + mixed[2][2] * mixed[2][2]) + 2.0 * (
        mixed[0][1] * mixed[1][0] + mixed[0][2] * mixed[2][0] + mixed[1][2] * mixed[2][1]
    )
    chtr = ch * trh
    ob[(2, i) + tile] = ob[(2, i) + tile] - chtr + al * (square + kk * kk * (1.0 / 3.0))
    chtr3 = chtr * (1.0 / 3.0)
    scale = alk - tdiv
    for p, (x, y) in enumerate(sym_pairs):
        if x == y:
            moved_g = 2.0 * total([g[pair_index[x][k]] * ds[x][k] for k in range(3)])
            moved_c = 2.0 * total([cv[pair_index[x][k]] * ds[x][k] for k in range(3)])
        else:
            moved_g = total([g[pair_index[x][k]] * ds[y][k] + g[pair_index[y][k]] * ds[x][k] for k in range(3)])
            moved_c = total([cv[pair_index[x][k]] * ds[y][k] + cv[pair_index[y][k]] * ds[x][k] for k in range(3)])
        ob[(3 + p, i) + tile] = ob[(3 + p, i) + tile] - al2 * cv[p] + moved_g - tdiv * g[p]
        product = total([mixed[x][k] * cv[pair_index[k][y]] for k in range(3)])
        ob[(9 + p, i) + tile] = ob[(9 + p, i) + tile] + scale * cv[p] - al2 * product + moved_c - ch * hess[p] + chtr3 * g[p]


def motion(fl, fine, jj):
    odd = jj & 1
    t = (jj + 1) >> 1
    u = t + 1 - 2 * odd
    lapse, shift, conf = [0.75 * fine[m, t] + 0.25 * fine[m, u] for m in range(3)]
    root = lax.rsqrt(conf)
    return lapse * fl[5, jj] - shift, lapse + jnp.abs(shift), lapse * (root * root * root) * fl[6, jj]


def split_flux(fl, fine, fpm, jj, given=None):
    moved, speed, weight = motion(fl, fine, jj) if given is None else given
    vel = fl[5, jj]
    plus = 0.5 * (moved + speed)
    minus = 0.5 * (moved - speed)
    half = 0.5 * weight
    extra = (None, half, None, None, half * vel)
    for n in range(5):
        v = fl[n, jj]
        fp, fm = v * plus, v * minus
        if extra[n] is not None:
            fp, fm = fp + extra[n], fm + extra[n]
        fpm[n, jj] = fp
        fpm[5 + n, jj] = fm


def cell_terms(v):
    e = [v[k + 1] - v[k] for k in range(len(v) - 1)]
    d, z0, z1, z2 = [None], [None], [None], [None]
    for k in range(1, len(v) - 1):
        dk = e[k] - e[k - 1]
        mid = e[k] + e[k - 1]
        square = dk * dk
        flat = mid * mid + 4e-6
        s1 = flat + (13.0 / 3.0) * square
        both = flat + (25.0 / 3.0) * square
        cross = (4.0 * dk) * mid
        s0, s2 = both + cross, both - cross
        d.append(dk)
        z0.append(s0 * s0)
        z1.append(s1 * s1)
        z2.append(s2 * s2)
    return d, z0, z1, z2


def correction(z0, z1, z2, d0, d1, d2):
    w0, w1, w2 = 1.0 / z0, 2.0 / z1, 1.0 / z2
    top = w0 * ((2.0 / 3.0) * d0 - d1) - (w1 * d1 + w2 * d2)
    return top * (1.0 / (w0 + 3.0 * (w1 + w2)))


def weno(fpm, oh, n, tile):
    layers = FINE + 6
    fp = [fpm[(n, k) + tile] for k in range(layers)]
    fm = [fpm[(5 + n, k) + tile] for k in range(layers)]
    dp, p0, p1, p2 = cell_terms(fp)
    dm, m0, m1, m2 = cell_terms(fm)
    last = None
    for k in range(2, layers - 3):
        face = (fp[k] + fm[k]) + (fp[k + 1] + fm[k + 1])
        face = face + correction(p0[k - 1], p1[k], p2[k + 1], dp[k - 1], dp[k], dp[k + 1])
        face = face + correction(m2[k + 2], m1[k + 1], m0[k], dm[k + 2], dm[k + 1], dm[k])
        if last is not None:
            oh[(n, k - 3) + tile] = last - face
        last = face


def iota2(shape, dim):
    return lax.broadcasted_iota(jnp.int32, shape, dim)


def refine_weights(fine_pos, coarse_pos, start):
    center = start + (fine_pos >> 1)
    side = center + 2 * (fine_pos & 1) - 1
    return jnp.where(coarse_pos == center, 0.75, jnp.where(coarse_pos == side, 0.25, 0.0)).astype(F32)


def thirds(v):
    high = v.astype(jnp.bfloat16)
    rest = v - high.astype(F32)
    mid = rest.astype(jnp.bfloat16)
    low = (rest - mid.astype(F32)).astype(jnp.bfloat16)
    return [high, mid, low]


def times(v, weights):
    return jnp.dot(jnp.concatenate(thirds(v), 1), weights, preferred_element_type=F32)


def applied(weights, v):
    return jnp.dot(weights, jnp.concatenate(thirds(v), 0), preferred_element_type=F32)


def make_fine(mp, fine, py, pz, layers):
    for m, f in enumerate((LAPSE, SHIFT, CONF)):
        coarse = jnp.concatenate([mp[f, 1 + t] for t in layers], 0)
        wide = times(coarse, pz[...])
        for part in range(0, len(layers), 4):
            block = applied(py[...], wide[CY * part : CY * (part + 4)])
            for k in range(4):
                fine[m, layers[part + k]] = block[CY * k : CY * (k + 1)]


def make_sources(fl, vyz, summed, src, plane, ry, rz):
    def pair(c, _):
        cells = []
        for s in range(2):
            j = 2 * c + s
            q = j + 3
            dot = fl[1, q] * fl[5, q] + fl[2, q] * vyz[0, j] + fl[3, q] * vyz[1, j]
            cells.append(fl[4, q] + fl[0, q] + dot + 3.0 * fl[6, q])
        summed[c] = cells[0] + cells[1]
        return 0

    lax.fori_loop(0, COARSE, pair, 0)
    level = times(summed[...].reshape(COARSE * CY, CZ), rz[...])
    level = applied(ry[...], level).reshape(COARSE, CY, CZ)
    src[1:COARSE] = level[: COARSE - 1]
    plane[...] = pltpu.roll(level[COARSE - 1], CZ - CZ // 4, 1)[CY // 4 : CY // 4 + CY // 2, : CZ // 2]


def kernel(sizes, lapse, conf, curv, metric, trace, shift, dens, mom, ener, vel, pres, ob, oh, mp, src,
           fl, vyz, plane, summed, dd, fine, fpm, py, pz, ry, rz, ysten, zsten, drift, lsem, ssem, rsem):
    stars, blocks = sizes
    count = stars * blocks
    blk = lax.axis_index("blk")
    me = lax.axis_index("star") * blocks + blk
    up = lax.rem(me + 1, count)
    down = lax.rem(me + count - 1, count)
    up = (up // blocks, lax.rem(up, blocks))
    down = (down // blocks, lax.rem(down, blocks))

    barrier = pltpu.get_barrier_semaphore()
    for device in (up, down):
        pl.semaphore_signal(barrier, inc=1, device_id=device, device_id_type=MESH)

    own = pl.ds(2, COARSE)
    fown = pl.ds(3, FINE)
    loads = [
        pltpu.make_async_copy(source, target, lsem.at[k])
        for k, (source, target) in enumerate((
            (dens.at[0], fl.at[0, fown]),
            (mom.at[0], fl.at[pl.ds(1, 3), fown]),
            (ener.at[0], fl.at[4, fown]),
            (vel.at[0, 0], fl.at[5, fown]),
            (pres.at[0], fl.at[6, fown]),
            (vel.at[0, pl.ds(1, 2)], vyz),
            (shift, mp.at[pl.ds(SHIFT, 3), own]),
            (lapse, mp.at[LAPSE, own]),
            (conf, mp.at[CONF, own]),
            (curv, mp.at[CURV, own]),
            (metric, mp.at[pl.ds(METRIC, 6), own]),
            (trace, mp.at[pl.ds(TRACE, 6), own]),
        ))
    ]
    def tile_at(t):
        return (pl.ds(pl.multiple_of((t >> 1) * 8, 8), 8), pl.ds(pl.multiple_of((t & 1) * LANES, LANES), LANES))

    def metric_layers(start, inner):
        derivatives(mp, ob, dd, src, ysten, zsten, start, inner)

        def pair(q, _):
            slot, y = q >> 1, q & 1
            for z in range(CZ // LANES):
                tile = (pl.ds(pl.multiple_of(8 * y, 8), 8), pl.ds(LANES * z, LANES))
                rates(mp, ob, dd, slot, start + slot, tile)
            return 0

        lax.fori_loop(0, 4, pair, 0)

    def inner(k, _):
        metric_layers(2 + 2 * k, True)
        return 0

    def first_part():
        for copy in loads:
            copy.start()

        def fill(ref, weights, shape, copies=3):
            part = weights(iota2(shape, 0), iota2(shape, 1)).astype(jnp.bfloat16)
            wide = ref.shape[1] != shape[1]
            for k in range(copies):
                if wide:
                    ref[:, shape[1] * k : shape[1] * k + shape[1]] = part
                else:
                    ref[shape[0] * k : shape[0] * k + shape[0], :] = part

        def in_block(r, c, weights):
            return jnp.where((r ^ c) < CY, weights, 0.0)

        fill(rz, lambda r, c: jnp.where(CZ // 4 + (r >> 1) == c, 0.125, 0.0), (CZ, CZ))
        fill(ry, lambda r, c: in_block(r, c, jnp.where(CY // 4 + ((c & CY - 1) >> 1) == (r & CY - 1), 1.0, 0.0)), (COARSE * CY, COARSE * CY))
        fill(zsten, lambda r, c: stencil(c, r, CZ), (CZ, CZ), 2)
        fill(ysten, lambda r, c: stencil(r, c, CY), (CY, CY), 2)
        fill(pz, lambda r, c: refine_weights(c, r, CZ // 4), (CZ, CZ))
        fill(py, lambda r, c: in_block(r, c, refine_weights(r & CY - 1, c & CY - 1, CY // 4)), (4 * CY, 4 * CY))

        for copy in loads[:6]:
            copy.wait()
        make_sources(fl, vyz, summed, src, plane, ry, rz)
        for copy in loads[6:9]:
            copy.wait()
        make_fine(mp, fine, py, pz, tuple(range(1, 1 + COARSE)))

        def flux_own(jj, _):
            split_flux(fl, fine, fpm, jj)
            return 0

        lax.fori_loop(3, FINE, flux_own, 0)
        for k, value in enumerate(motion(fl, fine, 4)):
            drift[0, k] = value

    def second_part():
        for copy in loads[9:]:
            copy.wait()
        lax.fori_loop(0, COARSE // 2 - 2, inner, 0)

    early = lax.rem(me, max(2, count // 16)) == 0

    @pl.when(early)
    def _():
        first_part()
        second_part()

    pl.semaphore_wait(barrier, 2)

    sends = []

    def send(source, target, device, when=None, loaded=None):
        k = len(sends)

        def copy_of(ref):
            return pltpu.make_async_remote_copy(
                src_ref=ref, dst_ref=target, send_sem=ssem.at[k], recv_sem=rsem.at[k], device_id=device, device_id_type=MESH
            )

        copy = copy_of(source)
        sends.append(copy)
        if loaded is not None:
            pl.when(early)(copy_of(loaded).start)
            pl.when(jnp.logical_not(early))(copy.start)
        elif when is None:
            copy.start()
        else:
            pl.when(when)(copy.start)
        return copy

    starts, ends = blk == 0, blk == blocks - 1
    continues_down, continues_up = jnp.logical_not(starts), jnp.logical_not(ends)

    top, bottom = pl.ds(COARSE - 2, 2), pl.ds(0, 2)
    low, high = pl.ds(0, 2), pl.ds(COARSE + 2, 2)
    ftop, flow, fhigh = pl.ds(FINE - 3, 3), pl.ds(0, 3), pl.ds(FINE + 3, 2)
    first = [
        send(shift.at[:, top], mp.at[pl.ds(SHIFT, 3), low], up, loaded=mp.at[pl.ds(SHIFT, 3), pl.ds(COARSE, 2)]),
        send(shift.at[:, bottom], mp.at[pl.ds(SHIFT, 3), high], down, loaded=mp.at[pl.ds(SHIFT, 3), pl.ds(2, 2)]),
        send(lapse.at[top], mp.at[LAPSE, low], up),
        send(lapse.at[bottom], mp.at[LAPSE, high], down),
        send(conf.at[top], mp.at[CONF, low], up),
        send(conf.at[bottom], mp.at[CONF, high], down),
    ]
    from_below, from_above = [], []
    pressure = lambda s: pres.at[0, s]
    for source, target in (
        (lambda s: dens.at[0, s], lambda s: fl.at[0, s]),
        (lambda s: mom.at[0, :, s], lambda s: fl.at[pl.ds(1, 3), s]),
        (lambda s: ener.at[0, s], lambda s: fl.at[4, s]),
        (lambda s: vel.at[0, 0, s], lambda s: fl.at[5, s]),
        (pressure, lambda s: fl.at[6, s]),
    ):
        from_below.append(send(source(ftop), target(flow), up, continues_up))
        if source is pressure:
            from_above.append(send(pres.at[0, pl.ds(0, 1)], fl.at[6, pl.ds(FINE + 3, 1)], down, continues_down))
        else:
            from_above.append(send(source(bottom), target(fhigh), down, continues_down))

    pl.when(jnp.logical_not(early))(first_part)
    from_above.append(send(fpm.at[pl.ds(5, 5), 5], fpm.at[pl.ds(5, 5), FINE + 5], down, continues_down))
    from_above.append(send(drift.at[0], drift.at[1], down, continues_down))
    third = [send(plane, src.at[0, pl.ds(0, CY // 2), pl.ds(0, CZ // 2)], up)]
    third += [
        send(curv.at[top], mp.at[CURV, low], up),
        send(curv.at[bottom], mp.at[CURV, high], down),
        send(metric.at[:, top], mp.at[pl.ds(METRIC, 6), low], up),
        send(metric.at[:, bottom], mp.at[pl.ds(METRIC, 6), high], down),
        send(trace.at[:, top], mp.at[pl.ds(TRACE, 6), low], up),
        send(trace.at[:, bottom], mp.at[pl.ds(TRACE, 6), high], down),
    ]
    pl.when(jnp.logical_not(early))(second_part)

    def outer(k, _):
        metric_layers(k * (COARSE - 2), False)
        return 0

    for copy in first:
        copy.wait_recv()
    lax.fori_loop(0, 2, outer, 0)
    make_fine(mp, fine, py, pz, (0, 1 + COARSE, 2 + COARSE, 2 + COARSE))
    for jj in range(FINE, FINE + 3):
        split_flux(fl, fine, fpm, jj)

    @pl.when(continues_down)
    def _():
        for copy in from_below:
            copy.wait_recv()
        for jj in range(3):
            split_flux(fl, fine, fpm, jj)

    @pl.when(starts)
    def _():
        fpm[:, :3] = jnp.zeros((10, 3, CY, CZ), F32)

    @pl.when(continues_up)
    def _():
        for copy in from_above:
            copy.wait_recv()
        split_flux(fl, fine, fpm, FINE + 3)
        split_flux(fl, fine, fpm, FINE + 4, [drift[1, k] for k in range(3)])

    @pl.when(ends)
    def _():
        fpm[:, FINE + 3 :] = jnp.zeros((10, 3, CY, CZ), F32)

    def faces(q, _):
        weno(fpm, oh, q >> 2, tile_at(q & 3))
        return 0

    lax.fori_loop(0, 20, faces, 0)

    for copy in first:
        copy.wait_send()

    @pl.when(continues_up)
    def _():
        for copy in from_below:
            copy.wait_send()

    @pl.when(continues_down)
    def _():
        for copy in from_above:
            copy.wait_send()

    for copy in third:
        copy.wait_recv()
    for copy in third:
        copy.wait_send()


def write_out(pb, ph, mp, src, ob, oh, edge, sem):
    copies = []

    def put(source, target):
        copy = pltpu.make_async_copy(source, target, sem.at[len(copies)])
        copy.start()
        copies.append(copy)

    rest = SHIFT - CURV
    middle = pl.ds(2, COARSE - 4)
    put(pb.at[pl.ds(CURV, rest), middle], ob.at[pl.ds(CURV, rest), middle])
    put(ph, oh.at[0])
    put(pb.at[pl.ds(0, CURV)], ob.at[pl.ds(0, CURV)])
    for k, i in enumerate((0, 1, COARSE - 2, COARSE - 1)):
        r = i + 2
        bx12 = mp[SHIFT, r] * (1.0 / 12.0)
        for f in range(CURV, SHIFT):
            moved = bx12 * x_first(mp, f, r)
            if f == CURV:
                source = src[i]
                if i == 0:
                    source = jnp.concatenate([source[: CY // 2, : CZ // 2], jnp.zeros((CY // 2, CZ // 2), F32)], 1)
                    around = jnp.zeros((CY // 4, CZ), F32)
                    source = jnp.concatenate([around, pltpu.roll(source, CZ // 4, 1), around], 0)
                moved = moved + (4.0 * math.pi) * mp[LAPSE, r] * source
            edge[f - CURV, k] = pb[f, i] + moved
        if k % 2:
            put(edge.at[:, pl.ds(k - 1, 2)], ob.at[pl.ds(CURV, rest), pl.ds(i - 1, 2)])
    for copy in copies:
        copy.wait()


def on_device(sizes, *arrays):
    hbm = pl.BlockSpec(memory_space=pltpu.HBM)
    vmem = pl.BlockSpec(memory_space=pltpu.VMEM)
    metric_out, fluid_out = (15, COARSE, CY, CZ), (5, FINE, CY, CZ)
    part = pl.pallas_call(
        functools.partial(kernel, sizes),
        out_shape=(
            pltpu.VMEM(metric_out, F32),
            pltpu.VMEM(fluid_out, F32),
            pltpu.VMEM((18, COARSE + 4, CY, CZ), F32),
            pltpu.VMEM((COARSE, CY, CZ), F32),
        ),
        in_specs=[hbm] * 11,
        out_specs=(vmem,) * 4,
        scratch_shapes=[
            pltpu.VMEM((7, FINE + 6, CY, CZ), F32),
            pltpu.VMEM((2, FINE, CY, CZ), F32),
            pltpu.VMEM((CY // 2, CZ // 2), F32),
            pltpu.VMEM((COARSE, CY, CZ), F32),
            pltpu.VMEM((2, 15, CY, CZ), F32),
            pltpu.VMEM((3, 12, CY, CZ), F32),
            pltpu.VMEM((10, FINE + 6, CY, CZ), F32),
            pltpu.VMEM((4 * CY, 3 * 4 * CY), jnp.bfloat16),
            pltpu.VMEM((3 * CZ, CZ), jnp.bfloat16),
            pltpu.VMEM((COARSE * CY, 3 * COARSE * CY), jnp.bfloat16),
            pltpu.VMEM((3 * CZ, CZ), jnp.bfloat16),
            pltpu.VMEM((CY, 2 * CY), jnp.bfloat16),
            pltpu.VMEM((2 * CZ, CZ), jnp.bfloat16),
            pltpu.VMEM((2, 3, CY, CZ), F32),
            pltpu.SemaphoreType.DMA((12,)),
            pltpu.SemaphoreType.DMA((25,)),
            pltpu.SemaphoreType.DMA((25,)),
        ],
        compiler_params=pltpu.CompilerParams(collective_id=0, has_side_effects=True, vmem_limit_bytes=54 << 20),
        cost_estimate=pl.CostEstimate(flops=60_000_000, bytes_accessed=8_000_000, transcendentals=0),
    )(*arrays)
    anywhere = pl.BlockSpec(memory_space=pl.ANY)
    return pl.pallas_call(
        write_out,
        out_shape=(jax.ShapeDtypeStruct(metric_out, F32), jax.ShapeDtypeStruct((1,) + fluid_out, F32)),
        in_specs=[vmem] * 4,
        out_specs=(anywhere, anywhere),
        scratch_shapes=[pltpu.VMEM((SHIFT - CURV, 4, CY, CZ), F32), pltpu.SemaphoreType.DMA((5,))],
        compiler_params=pltpu.CompilerParams(vmem_limit_bytes=16 << 20),
        cost_estimate=pl.CostEstimate(flops=0, bytes_accessed=6_400_000, transcendentals=0),
    )(*part)


def solution(mesh):
    level = P(("star", "blk"), None, None)
    level4 = P(None, ("star", "blk"), None, None)
    box = P("star", "blk", None, None)
    box5 = P("star", None, "blk", None, None)
    sizes = (mesh.shape["star"], mesh.shape["blk"])
    return jax.shard_map(
        functools.partial(on_device, sizes),
        mesh=mesh,
        in_specs=(level, level, level, level4, level4, level4, box, box5, box, box5, box),
        out_specs=(level4, box5),
        check_vma=False,
    )
```
